512 devices in a mesh: vc: 16 (over z, x_hi), vd: 32 (over x_lo, y, core).
Axes of the slice: x: 4 (x_hi: 2, x_lo: 2; x = x_hi * 2 + x_lo), y: 8, z: 8, core: 2. Of those that a mesh axis runs over, the one named last changes fastest.
Arguments:
- vectors_left: float32 [8, 1024, 4096], P(None, 'vc', 'vd'), may hold values from -0.8 to 0.8
- vectors_right: float32 [16, 1024, 4096], P(None, 'vd', 'vc'), may hold values from -0.8 to 0.8
- amplitudes: float32 [1024, 1024, 128], P('vc', 'vd'), may hold values from -0.005859375 to 0.005859375
Outputs:
- ladder: float32 [128, 8, 16], P('vd', None, 'vc')
The draws below stay inside these ranges and needn't reach their ends.
All inputs are finite; a program needn't handle non-finite values.
Results may differ from the reference program's by a relative error of at most 0.000094.
Values sent between devices are 32-bit elements; how exact they have to be, the bound alone decides.
No kernel may reach another device: no remote copies, remote signals or barrier semaphores. Data moves between devices by JAX's collectives and lax.ppermute only.
A program may use at most 64 MiB of HBM per device.

```python
import jax
import jax.numpy as jnp
from jax import lax

NV = 1024
NQ = 4096
NIJ = 128
NA = 8
NB = 16


def block_levels(rng, dims, shards, low, largest):
    def one(dim, parts):
        draws = jax.random.uniform(jax.random.fold_in(jax.random.fold_in(rng, 6), dim), (parts,), jnp.float32, low / len(shards), largest / len(shards))
        return jnp.repeat(jnp.exp(draws), dims[dim] // parts).reshape((-1,) + (1,) * (len(dims) - dim - 1))

    loudness = one(*shards[0])
    for cut in shards[1:]:
        loudness = loudness * one(*cut)
    return loudness


def noise(own_key, shape, deviation, reach, pieces=(), dtype=jnp.bfloat16):
    loudness = block_levels(own_key, shape, pieces, -0.22, 0.18) if pieces else 1.0
    values = jax.random.normal(own_key, shape, jnp.float32) * deviation * loudness
    return jnp.minimum(jnp.maximum(values, -reach), reach).astype(dtype)


def setup_inputs(seed: int = 0) -> dict:
    key_list = jax.random.split(jax.random.key(seed), 4)
    vectors_left = noise(key_list[0], (NA, NV, NQ), 0.134, 0.8, ((1, 16), (2, 32)), jnp.float32)
    vectors_right = noise(key_list[1], (NB, NV, NQ), 0.134, 0.8, ((1, 32), (2, 16)), jnp.float32)
    amplitudes = noise(key_list[2], (NV, NV, NIJ), (NV * NV) ** -0.5, 0.005859375, ((0, 16), (1, 32)), jnp.float32)
    return dict(vectors_left=vectors_left, vectors_right=vectors_right, amplitudes=amplitudes)


def reference(vectors_left, vectors_right, amplitudes):
    left_flat = vectors_left.reshape(NA * NV, NQ)
    right_flat = vectors_right.reshape(NB * NV, NQ)
    integrals = lax.dot_general(left_flat, right_flat, (((1,), (1,)), ((), ())), precision=lax.Precision.HIGHEST, preferred_element_type=jnp.float32)
    integrals = integrals.reshape(NA, NV, NB, NV)
    return jnp.einsum("acbd,cdi->iab", integrals, amplitudes, precision=lax.Precision.HIGHEST)
```

```python
import jax
import jax.numpy as jnp
from jax import lax
from jax.experimental import pallas as pl
from jax.experimental.pallas import tpu as pltpu
from jax.sharding import Mesh, PartitionSpec as P

AXES = ("z", "xh", "xl", "y", "core")
SIZES = (8, 2, 2, 8, 2)


def linear(z, xh, xl, y, core):
    return (((z % 8) * 2 + xh) * 2 + xl) * 16 + (y % 8) * 2 + core


def table(target):
    pairs = []
    for z in range(8):
        for xh in range(2):
            for xl in range(2):
                for y in range(8):
                    for core in range(2):
                        pairs.append((linear(z, xh, xl, y, core), linear(*target(z, xh, xl, y, core))))
    return pairs


SAME_XL = table(lambda z, xh, xl, y, core: (z, y % 2, xl, y // 2 * 2 + xh, core))
OTHER_XL = table(lambda z, xh, xl, y, core: (z, y % 2, 1 - xl, y // 2 * 2 + xh, core))
RING_X = table(lambda z, xh, xl, y, core: (z, xh, xl, y + 1 - 2 * core, core))
RING_Y = table(lambda z, xh, xl, y, core: (z, xh, xl, y - 1 + 2 * core, core))
SWAP_CORE = table(lambda z, xh, xl, y, core: (z, xh, xl, y, 1 - core))
SWAP_XH = table(lambda z, xh, xl, y, core: (z, 1 - xh, xl, y, core))


def send(array, pairs):
    return lax.ppermute(array, AXES, pairs)


def split(value):
    high = value.astype(jnp.bfloat16)
    low = (value - high.astype(jnp.float32)).astype(jnp.bfloat16)
    return high, low


def dot_nt(a, b):
    return lax.dot_general(a, b, (((1,), (1,)), ((), ())), preferred_element_type=jnp.float32)


def dot_nn(a, b):
    return lax.dot_general(a, b, (((1,), (0,)), ((), ())), preferred_element_type=jnp.float32)


def ladder_kernel(place, r_own, r_oth, lo0, lo1, lx0, lx1, t_own, t_oth, out, acc):
    step = pl.program_id(0)
    left_own = jnp.concatenate([lo0[...].reshape(8, 64, 128), lo1[...].reshape(8, 64, 128)], axis=1).reshape(1024, 128)
    left_oth = jnp.concatenate([lx0[...].reshape(8, 64, 128), lx1[...].reshape(8, 64, 128)], axis=1).reshape(1024, 128)
    left = jnp.concatenate([left_own, left_oth], axis=1)
    right = jnp.concatenate([r_own[...].reshape(512, 128), r_oth[...].reshape(512, 128)], axis=1)
    left_high, left_low = split(left)
    right_high, right_low = split(right)
    product = dot_nt(
        jnp.concatenate([right_high, right_high, right_low], axis=1),
        jnp.concatenate([left_high, left_low, left_high], axis=1),
    )

    for a in range(8):
        part = product[:, a * 128 : a * 128 + 128]

        @pl.when(step == 0)
        def _():
            acc[a] = part

        @pl.when(step > 0)
        def _():
            acc[a] += part

    @pl.when(step == 7)
    def _():
        total = jnp.zeros((128, 128), jnp.float32)
        for d in range(0, 32, 2):
            highs, lows, t_highs, t_lows = [], [], [], []
            for one in (d, d + 1):
                rows = jnp.concatenate([acc[a, pl.ds(one, 16, 32), :] for a in range(8)], axis=0)
                high, low = split(rows)
                highs.append(high)
                lows.append(low)
                for ref in (t_own, t_oth):
                    high, low = split(ref[:, one, :])
                    t_highs.append(high)
                    t_lows.append(low)
            total += dot_nn(
                jnp.concatenate(highs + highs + lows, axis=1),
                jnp.concatenate(t_highs + t_lows + t_highs, axis=0),
            )
        out[...] = total


def contract(place, right, left_own, left_oth, t_own, t_oth):
    def slot(place, y_wanted, sign):
        return lax.bitwise_and((place[0] - y_wanted) * sign + 8, 7)

    def left_map(half, sign):
        def index(step, place):
            parity = place[3] if half == 0 else 1 - place[3]
            wanted = 2 * lax.rem(step, 4) + parity
            order = lax.bitwise_xor(step // 4, place[2])
            return slot(place, wanted, place[1] * sign), order, 0, 0, 0

        return index

    left_block = (1, 1, 8, 64, 128)
    right_block = (1, 16, 32, 128)
    return pl.pallas_call(
        ladder_kernel,
        out_shape=jax.ShapeDtypeStruct((128, 128), jnp.float32),
        grid_spec=pltpu.PrefetchScalarGridSpec(
            num_scalar_prefetch=1,
            grid=(8,),
            in_specs=[
                pl.BlockSpec(right_block, lambda step, place: (step, 0, 0, place[4])),
                pl.BlockSpec(right_block, lambda step, place: (step, 0, 0, 1 - place[4])),
                pl.BlockSpec(left_block, left_map(0, 1)),
                pl.BlockSpec(left_block, left_map(1, 1)),
                pl.BlockSpec(left_block, left_map(0, -1)),
                pl.BlockSpec(left_block, left_map(1, -1)),
                pl.BlockSpec((64, 32, 128), lambda step, place: (0, 0, 0)),
                pl.BlockSpec((64, 32, 128), lambda step, place: (0, 0, 0)),
            ],
            out_specs=pl.BlockSpec((128, 128), lambda step, place: (0, 0)),
            scratch_shapes=[pltpu.VMEM((8, 512, 128), jnp.float32)],
        ),
        compiler_params=pltpu.CompilerParams(vmem_limit_bytes=40 * 1024 * 1024),
        cost_estimate=pl.CostEstimate(flops=6 << 30, bytes_accessed=16 << 20, transcendentals=0),
        name="ladder",
    )(place, right, right, left_own, left_own, left_oth, left_oth, t_own, t_oth)


def shards(vectors_left, vectors_right, amplitudes):
    y, core = lax.axis_index("y"), lax.axis_index("core")
    place = jnp.stack([y, 1 - 2 * core, lax.axis_index("xl"), lax.axis_index("xh"), core]).astype(jnp.int32)
    right = lax.all_gather(vectors_right, "z", axis=0)
    own = jnp.stack([send(vectors_left, SAME_XL), send(vectors_left, OTHER_XL)])
    ahead, behind = [own], []
    for step in range(4):
        ahead.append(send(ahead[-1], RING_X))
        if step < 3:
            behind.append(send(behind[-1] if behind else own, RING_Y))
    left_own = jnp.stack(ahead + behind[::-1])
    left_oth = send(left_own, SWAP_CORE)
    t_oth = send(amplitudes, SWAP_XH)
    partial = contract(place, right, left_own, left_oth, amplitudes, t_oth)
    partial = partial.reshape(8, 8, 2, 2, 8, 2, 4).transpose(2, 3, 5, 1, 4, 6, 0).reshape(8, 16, 128)
    near = lax.all_to_all(partial, ("xh", "xl", "core"), 0, 0, tiled=True)
    near = jnp.sum(near, axis=0).reshape(64, 32)
    far = lax.all_to_all(near, ("z", "y"), 0, 0, tiled=True)
    return jnp.sum(far, axis=0).reshape(4, 8, 1)


def solution(mesh):
    fine = Mesh(mesh.devices.reshape(SIZES), AXES)
    c_axes, d_axes = ("z", "xh"), ("xl", "y", "core")
    return jax.shard_map(
        shards,
        mesh=fine,
        in_specs=(P(None, c_axes, d_axes), P(None, d_axes, c_axes), P(c_axes, d_axes, None)),
        out_specs=P(d_axes, None, c_axes),
        check_vma=False,
    )
```

```python
import jax
import jax.numpy as jnp
from jax import lax
from jax.experimental import pallas as pl
from jax.experimental.pallas import tpu as pltpu
from jax.sharding import Mesh, PartitionSpec as P

AXES = ("z", "xh", "xl", "y", "core")
SIZES = (8, 2, 2, 8, 2)


def linear(z, xh, xl, y, core):
    return (((z % 8) * 2 + xh) * 2 + xl) * 16 + (y % 8) * 2 + core


def table(target):
    pairs = []
    for z in range(8):
        for xh in range(2):
            for xl in range(2):
                for y in range(8):
                    for core in range(2):
                        pairs.append((linear(z, xh, xl, y, core), linear(*target(z, xh, xl, y, core))))
    return pairs


SAME_XL = table(lambda z, xh, xl, y, core: (z, y % 2, xl, y // 2 * 2 + xh, core))
OTHER_XL = table(lambda z, xh, xl, y, core: (z, y % 2, 1 - xl, y // 2 * 2 + xh, core))
RING_X = table(lambda z, xh, xl, y, core: (z, xh, xl, y + 1 - 2 * core, core))
RING_Y = table(lambda z, xh, xl, y, core: (z, xh, xl, y - 1 + 2 * core, core))
SWAP_CORE = table(lambda z, xh, xl, y, core: (z, xh, xl, y, 1 - core))
SWAP_XH = table(lambda z, xh, xl, y, core: (z, 1 - xh, xl, y, core))


def send(array, pairs):
    return lax.ppermute(array, AXES, pairs)


def split(value):
    high = value.astype(jnp.bfloat16)
    low = (value - high.astype(jnp.float32)).astype(jnp.bfloat16)
    return high, low

def dot_nt(a, b):
    return lax.dot_general(a, b, (((1,), (1,)), ((), ())), preferred_element_type=jnp.float32)

def dot_nn(a, b):
    return lax.dot_general(a, b, (((1,), (0,)), ((), ())), preferred_element_type=jnp.float32)

PAIRS = (0, 1, 3, 2)
ARRIVAL = (0, 1, 7, 2, 6, 3, 5, 4)

def ladder_kernel(place, right, *refs):
    own, oth = refs[:8], refs[8:16]
    t_own, t_oth, out = refs[16:19]
    r_buf, l_buf, t_buf, r_mul, l_mul, acc, y_high, y_low, t_high, t_low, r_sem, l_sem, t_sem = refs[19:]
    y, sign, xl_here, xh, core = (place[i] for i in range(5))

    def pair(k):
        return lax.rem(y // 2 + PAIRS[k], 4)

    def right_copy(k, xl):
        return pltpu.make_async_copy(right.at[lax.bitwise_xor(xl, xl_here) * 4 + pair(k)], r_buf.at[2 * k + xl], r_sem.at[2 * k + xl])

    def left_copy(side, slot):
        at = lax.bitwise_and(y + (8 - slot if side == 0 else slot) * sign + 8, 7)
        return pltpu.make_async_copy((own, oth)[side][slot], l_buf.at[side, at], l_sem.at[side, at])

    def left_wait(side, at):
        pltpu.make_async_copy(own[0], l_buf.at[side, at], l_sem.at[side, at]).wait()

    for xl in range(2):
        right_copy(0, xl).start()
    for slot in ARRIVAL:
        left_copy(0, slot).start()
        left_copy(1, slot).start()
    for k in range(1, 4):
        for xl in range(2):
            right_copy(k, xl).start()
    t_copies = [pltpu.make_async_copy(ref, t_buf.at[i], t_sem.at[i]) for i, ref in enumerate((t_own, t_oth))]
    for copy in t_copies:
        copy.start()

    def prepare(k, part):
        xl, side = part // 2, part % 2
        if part == 0:
            for each in range(2):
                right_copy(k, each).wait()
                left_wait(each, 2 * pair(k))
                left_wait(each, 2 * pair(k) + 1)
        slot = k % 2
        lanes = jnp.where(side == 0, core, 1 - core) * 128
        value = r_buf[2 * k + xl, :, :, pl.ds(pl.multiple_of(lanes, 128), 128)].reshape(512, 128)
        high, low = split(value)
        at = part * 128
        r_mul[slot, :, at : at + 128] = high
        r_mul[slot, :, 512 + at : 512 + at + 128] = low
        for half, where in enumerate((2 * pair(k) + xh, 2 * pair(k) + 1 - xh)):
            high, low = split(l_buf[side, where, xl])
            l_mul[slot, :, half * 64 : half * 64 + 64, at : at + 128] = high
            l_mul[slot, :, half * 64 : half * 64 + 64, 512 + at : 512 + at + 128] = low

    def multiply(k, part):
        slot, a = k % 2, part * 2
        left = l_mul[slot, a : a + 2].reshape(256, 1024)
        both = r_mul[slot]
        product = dot_nt(
            jnp.concatenate([both, both[:, :512]], axis=1),
            jnp.concatenate([left[:, :512], left], axis=1),
        )
        for i in range(2):
            piece = product[:, i * 128 : i * 128 + 128]
            if k == 0:
                acc[a + i] = piece
            else:
                acc[a + i] += piece

    def prepare_t(d):
        for half in range(2):
            high, low = split(t_buf[half, pl.ds(d, 64, 32), :])
            t_high[d * 128 + half * 64 : d * 128 + half * 64 + 64, :] = high
            t_low[d * 128 + half * 64 : d * 128 + half * 64 + 64, :] = low

    for part in range(4):
        prepare(0, part)
    for k in range(4):
        if k == 1:
            for copy in t_copies:
                copy.wait()
        for part in range(4):
            multiply(k, part)
            if k < 3:
                prepare(k + 1, part)
            if k >= 1:
                for d in range((k - 1) * 12 + part * 3, min((k - 1) * 12 + part * 3 + 3, 32)):
                    prepare_t(d)
    for d in range(32):
        for a in range(8):
            high, low = split(acc[a, pl.ds(d, 16, 32), :])
            y_high[a * 16 : a * 16 + 16, d * 128 : d * 128 + 128] = high
            y_low[a * 16 : a * 16 + 16, d * 128 : d * 128 + 128] = low
    total = dot_nn(y_high[...], t_high[...]) + dot_nn(y_high[...], t_low[...]) + dot_nn(y_low[...], t_high[...])
    total = total.T
    for xl in range(2):
        for each in range(2):
            for row in range(8):
                first = xl * 64 + row * 8 + each * 4
                for xh_to in range(2):
                    out[xh_to * 4 + xl * 2 + each, row] = total[first : first + 4]

def contract(place, right, own, oth, t_own, t_oth):
    any_spec = pl.BlockSpec(memory_space=pl.ANY)
    return pl.pallas_call(
        ladder_kernel,
        out_shape=jax.ShapeDtypeStruct((8, 8, 4, 128), jnp.float32),
        in_specs=[pl.BlockSpec(memory_space=pltpu.SMEM)] + [any_spec] * 19,
        out_specs=pl.BlockSpec(memory_space=pltpu.VMEM),
        scratch_shapes=[
            pltpu.VMEM((8, 16, 32, 256), jnp.float32),
            pltpu.VMEM((2, 8, 2, 8, 64, 128), jnp.float32),
            pltpu.VMEM((2, 2048, 128), jnp.float32),
            pltpu.VMEM((2, 512, 1024), jnp.bfloat16),
            pltpu.VMEM((2, 8, 128, 1024), jnp.bfloat16),
            pltpu.VMEM((8, 512, 128), jnp.float32),
            pltpu.VMEM((128, 4096), jnp.bfloat16),
            pltpu.VMEM((128, 4096), jnp.bfloat16),
            pltpu.VMEM((4096, 128), jnp.bfloat16),
            pltpu.VMEM((4096, 128), jnp.bfloat16),
            pltpu.SemaphoreType.DMA((8,)),
            pltpu.SemaphoreType.DMA((2, 8)),
            pltpu.SemaphoreType.DMA((2,)),
        ],
        compiler_params=pltpu.CompilerParams(vmem_limit_bytes=56 * 1024 * 1024),
        cost_estimate=pl.CostEstimate(flops=6 << 30, bytes_accessed=16 << 20, transcendentals=0),
        name="ladder",
    )(place, right, *own, *oth, t_own.reshape(2048, 128), t_oth.reshape(2048, 128))


def after(array, *earlier):
    return lax.optimization_barrier((array, *earlier))[0]


def shards(vectors_left, vectors_right, amplitudes):
    z, xh, y, core = (lax.axis_index(name) for name in ("z", "xh", "y", "core"))
    place = jnp.stack([y, 1 - 2 * core, lax.axis_index("xl"), xh, core]).astype(jnp.int32)
    right = lax.all_gather(vectors_right, "z", axis=0)
    same, other = send(vectors_left, SAME_XL), send(vectors_left, OTHER_XL)
    own = jnp.stack([same, other])
    x1 = send(own, RING_X)
    t_oth = send(amplitudes, SWAP_XH)
    y1 = send(own, RING_Y)
    own_swapped = send(own, SWAP_CORE)
    x2 = send(x1, RING_X)
    y2 = send(after(y1, x1), RING_Y)
    x1_swapped = send(after(x1, own_swapped), SWAP_CORE)
    x3 = send(after(x2, y1), RING_X)
    y1_swapped = send(y1, SWAP_CORE)
    y3 = send(after(y2, x2), RING_Y)
    x2_swapped = send(x2, SWAP_CORE)
    x4 = send(after(x3, y2, t_oth), RING_X)
    y2_swapped = send(y2, SWAP_CORE)
    x3_swapped = send(x3, SWAP_CORE)
    y3_swapped = send(y3, SWAP_CORE)
    x4_swapped = send(x4, SWAP_CORE)
    left_own = [own, x1, x2, x3, x4, y3, y2, y1]
    left_oth = [own_swapped, x1_swapped, x2_swapped, x3_swapped, x4_swapped, y3_swapped, y2_swapped, y1_swapped]
    partial = contract(place, right, left_own, left_oth, amplitudes, t_oth)
    near = lax.all_to_all(partial, ("xh", "xl", "core"), 0, 0, tiled=True)
    near = jnp.broadcast_to(jnp.sum(near, axis=0)[None], (8, 8, 4, 128)).reshape(64, 4, 128)
    far = jnp.sum(lax.all_to_all(near, ("z", "y"), 0, 0, tiled=True), axis=0)
    return lax.dynamic_slice(far.reshape(4, 8, 16), (0, 0, z * 2 + xh), (4, 8, 1))


def solution(mesh):
    fine = Mesh(mesh.devices.reshape(SIZES), AXES)
    c_axes, d_axes = ("z", "xh"), ("xl", "y", "core")
    return jax.shard_map(
        shards,
        mesh=fine,
        in_specs=(P(None, c_axes, d_axes), P(None, d_axes, c_axes), P(c_axes, d_axes, None)),
        out_specs=P(d_axes, None, c_axes),
        check_vma=False,
    )
```

```python
import jax
import jax.numpy as jnp
from jax import lax
from jax.experimental import pallas as pl
from jax.experimental.pallas import tpu as pltpu
from jax.sharding import Mesh, PartitionSpec as P

AXES = ("z", "xh", "xl", "y", "core")
SIZES = (8, 2, 2, 8, 2)


def linear(z, xh, xl, y, core):
    return (((z % 8) * 2 + xh) * 2 + xl) * 16 + (y % 8) * 2 + core


def table(target):
    pairs = []
    for z in range(8):
        for xh in range(2):
            for xl in range(2):
                for y in range(8):
                    for core in range(2):
                        pairs.append((linear(z, xh, xl, y, core), linear(*target(z, xh, xl, y, core))))
    return pairs


SAME_XL = table(lambda z, xh, xl, y, core: (z, y % 2, xl, y // 2 * 2 + xh, core))
OTHER_XL = table(lambda z, xh, xl, y, core: (z, y % 2, 1 - xl, y // 2 * 2 + xh, core))
RING_X = table(lambda z, xh, xl, y, core: (z, xh, xl, y + 1 - 2 * core, core))
RING_Y = table(lambda z, xh, xl, y, core: (z, xh, xl, y - 1 + 2 * core, core))
SWAP_CORE = table(lambda z, xh, xl, y, core: (z, xh, xl, y, 1 - core))
SWAP_XH = table(lambda z, xh, xl, y, core: (z, 1 - xh, xl, y, core))
GROUPS = ((0, 1, 7, 2), (6, 3, 5, 4))
PAIRS = (0, 1, 3, 2)
IN_HBM = pl.BlockSpec(memory_space=pltpu.HBM)


def send(array, pairs):
    return lax.ppermute(array, AXES, pairs)


def after(array, *earlier):
    return lax.optimization_barrier((array, *earlier))[0]


def split(value):
    high = value.astype(jnp.bfloat16)
    low = (value - high.astype(jnp.float32)).astype(jnp.bfloat16)
    return high, low


def dot_nt(a, b):
    return lax.dot_general(a, b, (((1,), (1,)), ((), ())), preferred_element_type=jnp.float32)


def dot_nn(a, b):
    return lax.dot_general(a, b, (((1,), (0,)), ((), ())), preferred_element_type=jnp.float32)


def pieces_kernel(piece, out):
    high, low = split(piece[...])
    out[..., :128] = high
    out[..., 128:] = low


def split_pieces(group):
    count = group.shape[0]
    return pl.pallas_call(
        pieces_kernel,
        out_shape=pltpu.HBM((count, 2, 8, 64, 256), jnp.bfloat16),
        grid=(count, 2),
        in_specs=[pl.BlockSpec((1, 1, 8, 64, 128), lambda i, j: (i, j, 0, 0, 0))],
        out_specs=pl.BlockSpec((1, 1, 8, 64, 256), lambda i, j: (i, j, 0, 0, 0)),
        compiler_params=pltpu.CompilerParams(vmem_limit_bytes=8 * 1024 * 1024),
        cost_estimate=pl.CostEstimate(flops=1 << 20, bytes_accessed=4 << 20, transcendentals=0),
        name="split_pieces",
    )(group)


def amplitudes_kernel(t_own, t_oth, high_out, low_out):
    for d in range(32):
        for half, ref in enumerate((t_own, t_oth)):
            high, low = split(ref[pl.ds(d, 64, 32), :])
            high_out[d * 128 + half * 64 : d * 128 + half * 64 + 64, :] = high
            low_out[d * 128 + half * 64 : d * 128 + half * 64 + 64, :] = low


def split_amplitudes(t_own, t_oth):
    shape = pltpu.HBM((4096, 128), jnp.bfloat16)
    whole = pl.BlockSpec((4096, 128), lambda: (0, 0))
    return pl.pallas_call(
        amplitudes_kernel,
        out_shape=(shape, shape),
        out_specs=(whole, whole),
        compiler_params=pltpu.CompilerParams(vmem_limit_bytes=8 * 1024 * 1024),
        cost_estimate=pl.CostEstimate(flops=1 << 20, bytes_accessed=4 << 20, transcendentals=0),
        name="split_amplitudes",
    )(t_own.reshape(2048, 128), t_oth.reshape(2048, 128))


def ladder_kernel(place, right, own0, own1, oth0, oth1, t_high_in, t_low_in, out, r_buf, l_buf, t_high, t_low, acc, y_high, y_low, flip, r_sem, l_sem, t_sem):
    y, sign, xl_here, xh, core = (place[i] for i in range(5))

    def pair(k):
        return lax.rem(y // 2 + PAIRS[k], 4)

    def right_copy(k, order):
        where = lax.bitwise_xor(order, xl_here) * 4 + pair(k)
        return pltpu.make_async_copy(right.at[where], r_buf.at[k, order], r_sem.at[k, order])

    def left_copy(source, side, group, index):
        slot = GROUPS[group][index]
        at = lax.bitwise_and(y + (8 - slot if side == 0 else slot) * sign + 8, 7)
        half = lax.bitwise_xor(lax.bitwise_and(at, 1), xh)
        return pltpu.make_async_copy(
            source.at[index], l_buf.at[at // 2, side, half], l_sem.at[at // 2, side, half]
        )

    t_copies = [
        pltpu.make_async_copy(t_high_in, t_high, t_sem.at[0]),
        pltpu.make_async_copy(t_low_in, t_low, t_sem.at[1]),
    ]
    for order in range(2):
        right_copy(0, order).start()
    for group, sources in enumerate(((own0, oth0), (own1, oth1))):
        for index in range(4):
            for side in range(2):
                left_copy(sources[side], side, group, index).start()
        for k in (1, 2) if group == 0 else (3,):
            for order in range(2):
                right_copy(k, order).start()
    for copy in t_copies:
        copy.start()

    for k in range(4):
        for order in range(2):
            right_copy(k, order).wait()
        for side in range(2):
            for half in range(2):
                pltpu.make_async_copy(own0.at[0], l_buf.at[pair(k), side, half], l_sem.at[pair(k), side, half]).wait()
        r_high, r_low, l_high, l_low = [], [], [], []
        for order in range(2):
            high, low = split(r_buf[k, order].reshape(512, 256))
            r_high.append(high)
            r_low.append(low)
            for q_half in range(2):
                side = lax.bitwise_xor(core, q_half)
                both = jnp.concatenate([l_buf[pair(k), side, half, order] for half in range(2)], axis=1).reshape(1024, 256)
                l_high.append(both[:, :128])
                l_low.append(both[:, 128:])
        product = dot_nt(
            jnp.concatenate(r_high + r_low + r_high, axis=1),
            jnp.concatenate(l_high + l_high + l_low, axis=1),
        )
        for a in range(8):
            piece = product[:, a * 128 : a * 128 + 128]
            if k == 0:
                acc[a] = piece
            else:
                acc[a] += piece
    for copy in t_copies:
        copy.wait()
    for d in range(32):
        for a in range(8):
            high, low = split(acc[a, pl.ds(d, 16, 32), :])
            y_high[a * 16 : a * 16 + 16, d * 128 : d * 128 + 128] = high
            y_low[a * 16 : a * 16 + 16, d * 128 : d * 128 + 128] = low
    total = dot_nn(y_high[...], t_high[...]) + dot_nn(y_high[...], t_low[...]) + dot_nn(y_low[...], t_high[...])
    for a in range(8):
        flip[pl.ds(a, 16, 8), :] = total[a * 16 : a * 16 + 16]
    total = flip[...].T
    for xl in range(2):
        for each in range(2):
            for row in range(8):
                first = xl * 64 + row * 8 + each * 4
                for xh_to in range(2):
                    out[xh_to * 4 + xl * 2 + each, row * 4 : row * 4 + 4] = total[first : first + 4]


def contract(place, right, own, oth, t_split):
    return pl.pallas_call(
        ladder_kernel,
        out_shape=jax.ShapeDtypeStruct((8, 32, 128), jnp.float32),
        in_specs=[pl.BlockSpec(memory_space=pltpu.SMEM)] + [IN_HBM] * 7,
        out_specs=pl.BlockSpec(memory_space=pltpu.VMEM),
        scratch_shapes=[
            pltpu.VMEM((4, 2, 16, 32, 256), jnp.float32),
            pltpu.VMEM((4, 2, 2, 2, 8, 64, 256), jnp.bfloat16),
            pltpu.VMEM((4096, 128), jnp.bfloat16),
            pltpu.VMEM((4096, 128), jnp.bfloat16),
            pltpu.VMEM((8, 512, 128), jnp.float32),
            pltpu.VMEM((128, 4096), jnp.bfloat16),
            pltpu.VMEM((128, 4096), jnp.bfloat16),
            pltpu.VMEM((128, 128), jnp.float32),
            pltpu.SemaphoreType.DMA((4, 2)),
            pltpu.SemaphoreType.DMA((4, 2, 2)),
            pltpu.SemaphoreType.DMA((2,)),
        ],
        compiler_params=pltpu.CompilerParams(vmem_limit_bytes=60 * 1024 * 1024),
        cost_estimate=pl.CostEstimate(flops=6 << 30, bytes_accessed=16 << 20, transcendentals=0),
        name="ladder",
    )(place, right, *own, *oth, *t_split)


def pack_kernel(near, out, total):
    value = near[0]
    for part in range(1, 8):
        value += near[part]
    total[...] = value
    lane = lax.broadcasted_iota(jnp.int32, (8, 128), 1) // 16
    for z in range(8):
        packed = jnp.zeros((8, 128), jnp.float32)
        for k in range(4):
            rows = total[pl.ds(k, 8, 4), :]
            shift = (k - z) * 16 % 128
            packed = jnp.where(lane == k, pltpu.roll(rows, shift, 1) if shift else rows, packed)
        out[z * 8 : z * 8 + 8, :] = packed


def pack(near):
    return pl.pallas_call(
        pack_kernel,
        out_shape=jax.ShapeDtypeStruct((64, 128), jnp.float32),
        scratch_shapes=[pltpu.VMEM((32, 128), jnp.float32)],
        name="pack",
    )(near)


def shards(vectors_left, vectors_right, amplitudes):
    xh, y, core = (lax.axis_index(name) for name in ("xh", "y", "core"))
    place = jnp.stack([y, 1 - 2 * core, lax.axis_index("xl"), xh, core]).astype(jnp.int32)
    right = lax.all_gather(vectors_right, "z", axis=0)
    own = jnp.stack([send(vectors_left, SAME_XL), send(vectors_left, OTHER_XL)])
    x1 = send(own, RING_X)
    y1 = send(own, RING_Y)
    t_oth = send(amplitudes, SWAP_XH)
    x2 = send(x1, RING_X)
    y2 = send(after(y1, x1), RING_Y)
    own0 = jnp.stack([own, x1, y1, x2])
    oth0 = send(own0, SWAP_CORE)
    x3 = send(after(x2, y1), RING_X)
    y3 = send(after(y2, x2), RING_Y)
    x4 = send(after(x3, y2, t_oth), RING_X)
    own1 = jnp.stack([y2, x3, y3, x4])
    oth1 = send(own1, SWAP_CORE)
    t_split = split_amplitudes(amplitudes, t_oth)
    partial = contract(
        place, right, (split_pieces(own0), split_pieces(own1)), (split_pieces(oth0), split_pieces(oth1)), t_split
    )
    near = pack(lax.all_to_all(partial, ("xh", "xl", "core"), 0, 0, tiled=True))
    far = jnp.sum(lax.all_to_all(near, ("z", "y"), 0, 0, tiled=True), axis=0)
    return lax.dynamic_slice(far[:64].reshape(4, 2, 8), (0, xh, 0), (4, 1, 8)).reshape(4, 8, 1)


def solution(mesh):
    fine = Mesh(mesh.devices.reshape(SIZES), AXES)
    c_axes, d_axes = ("z", "xh"), ("xl", "y", "core")
    return jax.shard_map(
        shards,
        mesh=fine,
        in_specs=(P(None, c_axes, d_axes), P(None, d_axes, c_axes), P(c_axes, d_axes, None)),
        out_specs=P(d_axes, None, c_axes),
        check_vma=False,
    )
```

```python
import jax
import jax.numpy as jnp
from jax import lax
from jax.experimental import pallas as pl
from jax.experimental.pallas import tpu as pltpu
from jax.sharding import Mesh, PartitionSpec as P

AXES = ("z", "xh", "xl", "y", "core")
SIZES = (8, 2, 2, 8, 2)


def linear(z, xh, xl, y, core):
    return (((z % 8) * 2 + xh) * 2 + xl) * 16 + (y % 8) * 2 + core


def table(target):
    pairs = []
    for z in range(8):
        for xh in range(2):
            for xl in range(2):
                for y in range(8):
                    for core in range(2):
                        pairs.append((linear(z, xh, xl, y, core), linear(*target(z, xh, xl, y, core))))
    return pairs


SAME_XL = table(lambda z, xh, xl, y, core: (z, y % 2, xl, y // 2 * 2 + xh, core))
OTHER_XL = table(lambda z, xh, xl, y, core: (z, y % 2, 1 - xl, y // 2 * 2 + xh, core))
RING_X = table(lambda z, xh, xl, y, core: (z, xh, xl, y + 1 - 2 * core, core))
RING_Y = table(lambda z, xh, xl, y, core: (z, xh, xl, y - 1 + 2 * core, core))
SWAP_CORE = table(lambda z, xh, xl, y, core: (z, xh, xl, y, 1 - core))
SWAP_XH = table(lambda z, xh, xl, y, core: (z, 1 - xh, xl, y, core))
PAIRS = (0, 1, 3, 2)
NEEDED = ((0, 1, 7), (2, 6, 3, 5), (4,), ())


def send(array, pairs):
    return lax.ppermute(array, AXES, pairs)


def after(array, *earlier):
    return lax.optimization_barrier((array, *earlier))[0]


def split(value):
    high = value.astype(jnp.bfloat16)
    low = (value - high.astype(jnp.float32)).astype(jnp.bfloat16)
    return high, low


def dot_nt(a, b):
    return lax.dot_general(a, b, (((1,), (1,)), ((), ())), preferred_element_type=jnp.float32)


def dot_nn(a, b):
    return lax.dot_general(a, b, (((1,), (0,)), ((), ())), preferred_element_type=jnp.float32)


def amplitudes_kernel(t_own, t_oth, high_out, low_out):
    for d in range(32):
        for half, ref in enumerate((t_own, t_oth)):
            high, low = split(ref[pl.ds(d, 64, 32), :])
            high_out[d * 128 + half * 64 : d * 128 + half * 64 + 64, :] = high
            low_out[d * 128 + half * 64 : d * 128 + half * 64 + 64, :] = low


def split_amplitudes(t_own, t_oth):
    shape = jax.ShapeDtypeStruct((4096, 128), jnp.bfloat16)
    return pl.pallas_call(
        amplitudes_kernel,
        out_shape=(shape, shape),
        compiler_params=pltpu.CompilerParams(vmem_limit_bytes=8 * 1024 * 1024),
        cost_estimate=pl.CostEstimate(flops=1 << 20, bytes_accessed=4 << 20, transcendentals=0),
        name="split_amplitudes",
    )(t_own.reshape(2048, 128), t_oth.reshape(2048, 128))


def ladder_kernel(place, right, *refs):
    pieces, (t_high_in, t_low_in, out) = (refs[:8], refs[8:16]), refs[16:19]
    r_buf, raw, parts, t_high, t_low, acc, y_high, y_low, flip, r_sem, l_sem, t_sem = refs[19:]
    y, sign, xl_here, xh, core = (place[i] for i in range(5))

    def pair(k):
        return lax.rem(y // 2 + PAIRS[k], 4)

    def right_copy(k, order):
        where = lax.bitwise_xor(order, xl_here) * 4 + pair(k)
        return pltpu.make_async_copy(right.at[where], r_buf.at[k, order], r_sem.at[k, order])

    def left_copy(side, slot):
        return pltpu.make_async_copy(pieces[side][slot], raw.at[side, slot], l_sem.at[side, slot])

    def left(k, q_half, half, order):
        at = 2 * pair(k) + lax.bitwise_xor(half, xh)
        steps = (y - at) * sign
        side = lax.bitwise_xor(core, q_half)
        slot = lax.bitwise_and(8 + steps - 2 * side * steps, 7)
        return parts[side, slot, order]

    t_copies = [
        pltpu.make_async_copy(t_high_in, t_high, t_sem.at[0]),
        pltpu.make_async_copy(t_low_in, t_low, t_sem.at[1]),
    ]
    for k in range(4):
        for slot in NEEDED[k]:
            for side in range(2):
                left_copy(side, slot).start()
        for order in range(2):
            right_copy(k, order).start()
    for copy in t_copies:
        copy.start()
    for k in range(4):
        for slot in NEEDED[k]:
            for side in range(2):
                left_copy(side, slot).wait()
                high, low = split(raw[side, slot])
                parts[side, slot, :, :, :, :128] = high
                parts[side, slot, :, :, :, 128:] = low
        for order in range(2):
            right_copy(k, order).wait()
        r_high, r_low, l_high, l_low = [], [], [], []
        for order in range(2):
            high, low = split(r_buf[k, order].reshape(512, 256))
            r_high.append(high)
            r_low.append(low)
            for q_half in range(2):
                both = jnp.concatenate([left(k, q_half, half, order) for half in range(2)], axis=1).reshape(1024, 256)
                l_high.append(both[:, :128])
                l_low.append(both[:, 128:])
        product = dot_nt(
            jnp.concatenate(r_high + r_low + r_high, axis=1),
            jnp.concatenate(l_high + l_high + l_low, axis=1),
        )
        for a in range(8):
            piece = product[:, a * 128 : a * 128 + 128]
            if k == 0:
                acc[a] = piece
            else:
                acc[a] += piece
    for copy in t_copies:
        copy.wait()
    for d in range(32):
        for a in range(8):
            high, low = split(acc[a, pl.ds(d, 16, 32), :])
            y_high[a * 16 : a * 16 + 16, d * 128 : d * 128 + 128] = high
            y_low[a * 16 : a * 16 + 16, d * 128 : d * 128 + 128] = low
    total = dot_nn(y_high[...], t_high[...]) + dot_nn(y_high[...], t_low[...]) + dot_nn(y_low[...], t_high[...])
    for a in range(8):
        flip[pl.ds(a, 16, 8), :] = total[a * 16 : a * 16 + 16]
    total = flip[...].T
    for xl in range(2):
        for each in range(2):
            for row in range(8):
                first = xl * 64 + row * 8 + each * 4
                for xh_to in range(2):
                    out[xh_to * 4 + xl * 2 + each, row * 4 : row * 4 + 4] = total[first : first + 4]


def contract(place, right, own, oth, t_split):
    return pl.pallas_call(
        ladder_kernel,
        out_shape=jax.ShapeDtypeStruct((8, 32, 128), jnp.float32),
        in_specs=[pl.BlockSpec(memory_space=pltpu.SMEM)] + [pl.BlockSpec(memory_space=pl.ANY)] * 19,
        out_specs=pl.BlockSpec(memory_space=pltpu.VMEM),
        scratch_shapes=[
            pltpu.VMEM((4, 2, 16, 32, 256), jnp.float32),
            pltpu.VMEM((2, 8, 2, 8, 64, 128), jnp.float32),
            pltpu.VMEM((2, 8, 2, 8, 64, 256), jnp.bfloat16),
            pltpu.VMEM((4096, 128), jnp.bfloat16),
            pltpu.VMEM((4096, 128), jnp.bfloat16),
            pltpu.VMEM((8, 512, 128), jnp.float32),
            pltpu.VMEM((128, 4096), jnp.bfloat16),
            pltpu.VMEM((128, 4096), jnp.bfloat16),
            pltpu.VMEM((128, 128), jnp.float32),
            pltpu.SemaphoreType.DMA((4, 2)),
            pltpu.SemaphoreType.DMA((2, 8)),
            pltpu.SemaphoreType.DMA((2,)),
        ],
        compiler_params=pltpu.CompilerParams(vmem_limit_bytes=60 * 1024 * 1024),
        cost_estimate=pl.CostEstimate(flops=6 << 30, bytes_accessed=16 << 20, transcendentals=0),
        name="ladder",
    )(place, right, *own, *oth, *t_split)


def pack_kernel(near, out, total):
    value = near[0]
    for part in range(1, 8):
        value += near[part]
    total[...] = value
    lane = lax.broadcasted_iota(jnp.int32, (8, 128), 1) // 16
    for z in range(8):
        packed = jnp.zeros((8, 128), jnp.float32)
        for k in range(4):
            rows = total[pl.ds(k, 8, 4), :]
            shift = (k - z) * 16 % 128
            packed = jnp.where(lane == k, pltpu.roll(rows, shift, 1) if shift else rows, packed)
        out[z * 8 : z * 8 + 8, :] = packed


def pack(near):
    return pl.pallas_call(
        pack_kernel,
        out_shape=jax.ShapeDtypeStruct((64, 128), jnp.float32),
        scratch_shapes=[pltpu.VMEM((32, 128), jnp.float32)],
        name="pack",
    )(near)


def shards(vectors_left, vectors_right, amplitudes):
    xh, y, core = (lax.axis_index(name) for name in ("xh", "y", "core"))
    place = jnp.stack([y, 1 - 2 * core, lax.axis_index("xl"), xh, core]).astype(jnp.int32)
    right = lax.all_gather(vectors_right, "z", axis=0)
    own = jnp.stack([send(vectors_left, SAME_XL), send(vectors_left, OTHER_XL)])
    t_oth = send(amplitudes, SWAP_XH)
    x1 = send(own, RING_X)
    y1 = send(own, RING_Y)
    x2 = send(x1, RING_X)
    y2 = send(after(y1, x1), RING_Y)
    x3 = send(after(x2, y1, t_oth), RING_X)
    y3 = send(after(y2, x2), RING_Y)
    x4 = send(after(x3, y2), RING_X)
    left_own = [own, x1, x2, x3, x4, y3, y2, y1]
    t_split = split_amplitudes(amplitudes, t_oth)
    left_oth = [send(after(piece, *t_split) if piece is y3 else piece, SWAP_CORE) for piece in left_own]
    partial = contract(place, right, left_own, left_oth, t_split)
    near = pack(lax.all_to_all(partial, ("xh", "xl", "core"), 0, 0, tiled=True))
    far = jnp.sum(lax.all_to_all(near, ("z", "y"), 0, 0, tiled=True), axis=0)
    return lax.dynamic_slice(far[:64].reshape(4, 2, 8), (0, xh, 0), (4, 1, 8)).reshape(4, 8, 1)


def solution(mesh):
    fine = Mesh(mesh.devices.reshape(SIZES), AXES)
    c_axes, d_axes = ("z", "xh"), ("xl", "y", "core")
    return jax.shard_map(
        shards,
        mesh=fine,
        in_specs=(P(None, c_axes, d_axes), P(None, d_axes, c_axes), P(c_axes, d_axes, None)),
        out_specs=P(d_axes, None, c_axes),
        check_vma=False,
    )
```

```python
import jax
import jax.numpy as jnp
from jax import lax
from jax.experimental import pallas as pl
from jax.experimental.pallas import tpu as pltpu
from jax.sharding import Mesh, PartitionSpec as P

AXES = ("z", "xh", "xl", "y", "core")
SIZES = (8, 2, 2, 8, 2)


def linear(z, xh, xl, y, core):
    return (((z % 8) * 2 + xh) * 2 + xl) * 16 + (y % 8) * 2 + core


def table(target):
    pairs = []
    for z in range(8):
        for xh in range(2):
            for xl in range(2):
                for y in range(8):
                    for core in range(2):
                        pairs.append((linear(z, xh, xl, y, core), linear(*target(z, xh, xl, y, core))))
    return pairs


SAME_XL = table(lambda z, xh, xl, y, core: (z, y % 2, xl, y // 2 * 2 + xh, core))
OTHER_XL = table(lambda z, xh, xl, y, core: (z, y % 2, 1 - xl, y // 2 * 2 + xh, core))
RING_X = table(lambda z, xh, xl, y, core: (z, xh, xl, y + 1 - 2 * core, core))
RING_Y = table(lambda z, xh, xl, y, core: (z, xh, xl, y - 1 + 2 * core, core))
SWAP_CORE = table(lambda z, xh, xl, y, core: (z, xh, xl, y, 1 - core))
SWAP_XH = table(lambda z, xh, xl, y, core: (z, 1 - xh, xl, y, core))
PAIRS = (0, 1, 3, 2)
NEEDED = ((0, 1, 7), (2, 6, 3, 5), (4,), ())


def send(array, pairs):
    return lax.ppermute(array, AXES, pairs)


def after(array, *earlier):
    return lax.optimization_barrier((array, *earlier))[0]


def split(value):
    high = value.astype(jnp.bfloat16)
    low = (value - high.astype(jnp.float32)).astype(jnp.bfloat16)
    return high, low


def dot_nt(a, b):
    return lax.dot_general(a, b, (((1,), (1,)), ((), ())), preferred_element_type=jnp.float32)


def dot_nn(a, b):
    return lax.dot_general(a, b, (((1,), (0,)), ((), ())), preferred_element_type=jnp.float32)


def amplitudes_kernel(t_own, t_oth, high_out, low_out, first, second, t_high, t_low, in_sem, out_sem):
    blocks = ((t_own, first), (t_oth, second))
    copies = [pltpu.make_async_copy(ref, buf, in_sem.at[half]) for half, (ref, buf) in enumerate(blocks)]
    for copy in copies:
        copy.start()
    for half, (_, buf) in enumerate(blocks):
        copies[half].wait()
        for d in range(32):
            high, low = split(buf[pl.ds(d, 64, 32), :])
            t_high[d * 128 + half * 64 : d * 128 + half * 64 + 64, :] = high
            t_low[d * 128 + half * 64 : d * 128 + half * 64 + 64, :] = low
    results = [
        pltpu.make_async_copy(t_high, high_out, out_sem.at[0]),
        pltpu.make_async_copy(t_low, low_out, out_sem.at[1]),
    ]
    for copy in results:
        copy.start()
    for copy in results:
        copy.wait()


def split_amplitudes(t_own, t_oth):
    shape = pltpu.HBM((4096, 128), jnp.bfloat16)
    anywhere = pl.BlockSpec(memory_space=pl.ANY)
    return pl.pallas_call(
        amplitudes_kernel,
        out_shape=(shape, shape),
        in_specs=[anywhere] * 2,
        out_specs=[pl.BlockSpec(memory_space=pltpu.HBM)] * 2,
        scratch_shapes=[pltpu.VMEM((2048, 128), jnp.float32)] * 2
        + [pltpu.VMEM((4096, 128), jnp.bfloat16)] * 2
        + [pltpu.SemaphoreType.DMA((2,))] * 2,
        compiler_params=pltpu.CompilerParams(vmem_limit_bytes=8 * 1024 * 1024),
        cost_estimate=pl.CostEstimate(flops=1 << 20, bytes_accessed=4 << 20, transcendentals=0),
        name="split_amplitudes",
    )(*(pltpu.with_memory_space_constraint(block.reshape(2048, 128), pltpu.HBM) for block in (t_own, t_oth)))


def ladder_kernel(place, right, *refs):
    pieces, (t_high_in, t_low_in, out) = (refs[:8], refs[8:16]), refs[16:19]
    r_buf, raw, parts, t_high, t_low, acc, y_high, y_low, flip, r_sem, l_sem, t_sem = refs[19:]
    y, sign, xl_here, xh, core = (place[i] for i in range(5))

    def pair(k):
        return lax.rem(y // 2 + PAIRS[k], 4)

    def right_copy(k, order):
        where = lax.bitwise_xor(order, xl_here) * 4 + pair(k)
        return pltpu.make_async_copy(right.at[where], r_buf.at[k, order], r_sem.at[k, order])

    def left_copy(side, slot):
        return pltpu.make_async_copy(pieces[side][slot], raw.at[side, slot], l_sem.at[side, slot])

    def left(k, q_half, half, order):
        at = 2 * pair(k) + lax.bitwise_xor(half, xh)
        steps = (y - at) * sign
        side = lax.bitwise_xor(core, q_half)
        slot = lax.bitwise_and(8 + steps - 2 * side * steps, 7)
        return parts[side, slot, order]

    t_copies = [
        pltpu.make_async_copy(t_high_in, t_high, t_sem.at[0]),
        pltpu.make_async_copy(t_low_in, t_low, t_sem.at[1]),
    ]
    for k in range(4):
        for slot in NEEDED[k]:
            for side in range(2):
                left_copy(side, slot).start()
        for order in range(2):
            right_copy(k, order).start()
    for copy in t_copies:
        copy.start()
    for k in range(4):
        for slot in NEEDED[k]:
            for side in range(2):
                left_copy(side, slot).wait()
                high, low = split(raw[side, slot])
                parts[side, slot, :, :, :, :128] = high
                parts[side, slot, :, :, :, 128:] = low
        for order in range(2):
            right_copy(k, order).wait()
        r_high, r_low, l_high, l_low = [], [], [], []
        for order in range(2):
            high, low = split(r_buf[k, order].reshape(512, 256))
            r_high.append(high)
            r_low.append(low)
            for q_half in range(2):
                both = jnp.concatenate([left(k, q_half, half, order) for half in range(2)], axis=1).reshape(1024, 256)
                l_high.append(both[:, :128])
                l_low.append(both[:, 128:])
        product = dot_nt(
            jnp.concatenate(r_high + r_low + r_high, axis=1),
            jnp.concatenate(l_high + l_high + l_low, axis=1),
        )
        for a in range(8):
            piece = product[:, a * 128 : a * 128 + 128]
            if k == 0:
                acc[a] = piece
            else:
                acc[a] += piece
    for copy in t_copies:
        copy.wait()
    for d in range(32):
        for a in range(8):
            high, low = split(acc[a, pl.ds(d, 16, 32), :])
            y_high[a * 16 : a * 16 + 16, d * 128 : d * 128 + 128] = high
            y_low[a * 16 : a * 16 + 16, d * 128 : d * 128 + 128] = low
    total = dot_nn(y_high[...], t_high[...]) + dot_nn(y_high[...], t_low[...]) + dot_nn(y_low[...], t_high[...])
    for a in range(8):
        flip[pl.ds(a, 16, 8), :] = total[a * 16 : a * 16 + 16]
    total = flip[...].T
    for xl in range(2):
        for each in range(2):
            for row in range(8):
                first = xl * 64 + row * 8 + each * 4
                for xh_to in range(2):
                    out[xh_to * 4 + xl * 2 + each, row * 4 : row * 4 + 4] = total[first : first + 4]


def contract(place, right, own, oth, t_split):
    return pl.pallas_call(
        ladder_kernel,
        out_shape=jax.ShapeDtypeStruct((8, 32, 128), jnp.float32),
        in_specs=[pl.BlockSpec(memory_space=pltpu.SMEM)] + [pl.BlockSpec(memory_space=pl.ANY)] * 19,
        out_specs=pl.BlockSpec(memory_space=pltpu.VMEM),
        scratch_shapes=[
            pltpu.VMEM((4, 2, 16, 32, 256), jnp.float32),
            pltpu.VMEM((2, 8, 2, 8, 64, 128), jnp.float32),
            pltpu.VMEM((2, 8, 2, 8, 64, 256), jnp.bfloat16),
            pltpu.VMEM((4096, 128), jnp.bfloat16),
            pltpu.VMEM((4096, 128), jnp.bfloat16),
            pltpu.VMEM((8, 512, 128), jnp.float32),
            pltpu.VMEM((128, 4096), jnp.bfloat16),
            pltpu.VMEM((128, 4096), jnp.bfloat16),
            pltpu.VMEM((128, 128), jnp.float32),
            pltpu.SemaphoreType.DMA((4, 2)),
            pltpu.SemaphoreType.DMA((2, 8)),
            pltpu.SemaphoreType.DMA((2,)),
        ],
        compiler_params=pltpu.CompilerParams(vmem_limit_bytes=60 * 1024 * 1024),
        cost_estimate=pl.CostEstimate(flops=6 << 30, bytes_accessed=16 << 20, transcendentals=0),
        name="ladder",
    )(place, right, *own, *oth, *t_split)


def pack_kernel(near, out, total):
    value = near[0]
    for part in range(1, 8):
        value += near[part]
    total[...] = value
    lane = lax.broadcasted_iota(jnp.int32, (8, 128), 1) // 16
    for z in range(8):
        packed = jnp.zeros((8, 128), jnp.float32)
        for k in range(4):
            rows = total[pl.ds(k, 8, 4), :]
            shift = (k - z) * 16 % 128
            packed = jnp.where(lane == k, pltpu.roll(rows, shift, 1) if shift else rows, packed)
        out[z * 8 : z * 8 + 8, :] = packed


def pack(near):
    return pl.pallas_call(
        pack_kernel,
        out_shape=jax.ShapeDtypeStruct((64, 128), jnp.float32),
        scratch_shapes=[pltpu.VMEM((32, 128), jnp.float32)],
        name="pack",
    )(near)


def shards(vectors_left, vectors_right, amplitudes):
    xh, y, core = (lax.axis_index(name) for name in ("xh", "y", "core"))
    place = jnp.stack([y, 1 - 2 * core, lax.axis_index("xl"), xh, core]).astype(jnp.int32)
    right = lax.all_gather(vectors_right, "z", axis=0)
    own = jnp.stack([send(vectors_left, SAME_XL), send(vectors_left, OTHER_XL)])
    x1 = send(own, RING_X)
    t_oth = send(amplitudes, SWAP_XH)
    y1 = send(own, RING_Y)
    x2 = send(x1, RING_X)
    y2 = send(after(y1, x1), RING_Y)
    x3 = send(after(x2, y1), RING_X)
    y3 = send(after(y2, x2), RING_Y)
    x4 = send(after(x3, y2, t_oth), RING_X)
    t_split = split_amplitudes(amplitudes, t_oth)
    left_own = [own, x1, x2, x3, x4, y3, y2, y1]
    left_oth = [send(after(piece, *t_split) if piece is y3 else piece, SWAP_CORE) for piece in left_own]
    partial = contract(place, right, left_own, left_oth, t_split)
    near = pack(lax.all_to_all(partial, ("xh", "xl", "core"), 0, 0, tiled=True))
    far = jnp.sum(lax.all_to_all(near, ("z", "y"), 0, 0, tiled=True), axis=0)
    return lax.dynamic_slice(far[:64].reshape(4, 2, 8), (0, xh, 0), (4, 1, 8)).reshape(4, 8, 1)


def solution(mesh):
    fine = Mesh(mesh.devices.reshape(SIZES), AXES)
    c_axes, d_axes = ("z", "xh"), ("xl", "y", "core")
    return jax.shard_map(
        shards,
        mesh=fine,
        in_specs=(P(None, c_axes, d_axes), P(None, d_axes, c_axes), P(c_axes, d_axes, None)),
        out_specs=P(d_axes, None, c_axes),
        check_vma=False,
    )
```

```python
import jax
import jax.numpy as jnp
from jax import lax
from jax.experimental import pallas as pl
from jax.experimental.pallas import tpu as pltpu
from jax.sharding import Mesh, PartitionSpec as P

AXES = ("z", "xh", "xl", "y", "core")
SIZES = (8, 2, 2, 8, 2)


def linear(z, xh, xl, y, core):
    return (((z % 8) * 2 + xh) * 2 + xl) * 16 + (y % 8) * 2 + core


def table(target):
    pairs = []
    for z in range(8):
        for xh in range(2):
            for xl in range(2):
                for y in range(8):
                    for core in range(2):
                        pairs.append((linear(z, xh, xl, y, core), linear(*target(z, xh, xl, y, core))))
    return pairs


SAME_XL = table(lambda z, xh, xl, y, core: (z, y % 2, xl, y // 2 * 2 + xh, core))
OTHER_XL = table(lambda z, xh, xl, y, core: (z, y % 2, 1 - xl, y // 2 * 2 + xh, core))
RING_X = table(lambda z, xh, xl, y, core: (z, xh, xl, y + 1 - 2 * core, core))
RING_Y = table(lambda z, xh, xl, y, core: (z, xh, xl, y - 1 + 2 * core, core))
SWAP_CORE = table(lambda z, xh, xl, y, core: (z, xh, xl, y, 1 - core))
SWAP_XH = table(lambda z, xh, xl, y, core: (z, 1 - xh, xl, y, core))
GROUPS = ((0, 1, 7, 2), (6, 3, 5), (4,))
PAIRS = (0, 1, 3, 2)
NEEDED = ((0, 1, 7), (2, 6, 3, 5), (4,), ())


def send(array, pairs):
    return lax.ppermute(array, AXES, pairs)


def after(array, *earlier):
    return lax.optimization_barrier((array, *earlier))[0]


def split(value):
    high = value.astype(jnp.bfloat16)
    low = (value - high.astype(jnp.float32)).astype(jnp.bfloat16)
    return high, low


def dot_nt(a, b):
    return lax.dot_general(a, b, (((1,), (1,)), ((), ())), preferred_element_type=jnp.float32)


def dot_nn(a, b):
    return lax.dot_general(a, b, (((1,), (0,)), ((), ())), preferred_element_type=jnp.float32)


def amplitudes_kernel(t_own, t_oth, high_out, low_out, first, second, t_high, t_low, in_sem, out_sem):
    blocks = ((t_own, first), (t_oth, second))
    copies = [pltpu.make_async_copy(ref, buf, in_sem.at[half]) for half, (ref, buf) in enumerate(blocks)]
    for copy in copies:
        copy.start()
    for half, (_, buf) in enumerate(blocks):
        copies[half].wait()
        for d in range(32):
            high, low = split(buf[pl.ds(d, 64, 32), :])
            t_high[d * 128 + half * 64 : d * 128 + half * 64 + 64, :] = high
            t_low[d * 128 + half * 64 : d * 128 + half * 64 + 64, :] = low
    results = [
        pltpu.make_async_copy(t_high, high_out, out_sem.at[0]),
        pltpu.make_async_copy(t_low, low_out, out_sem.at[1]),
    ]
    for copy in results:
        copy.start()
    for copy in results:
        copy.wait()


def split_amplitudes(t_own, t_oth):
    shape = pltpu.HBM((4096, 128), jnp.bfloat16)
    anywhere = pl.BlockSpec(memory_space=pl.ANY)
    return pl.pallas_call(
        amplitudes_kernel,
        out_shape=(shape, shape),
        in_specs=[anywhere] * 2,
        out_specs=[pl.BlockSpec(memory_space=pltpu.HBM)] * 2,
        scratch_shapes=[pltpu.VMEM((2048, 128), jnp.float32)] * 2
        + [pltpu.VMEM((4096, 128), jnp.bfloat16)] * 2
        + [pltpu.SemaphoreType.DMA((2,))] * 2,
        compiler_params=pltpu.CompilerParams(vmem_limit_bytes=8 * 1024 * 1024),
        cost_estimate=pl.CostEstimate(flops=1 << 20, bytes_accessed=4 << 20, transcendentals=0),
        name="split_amplitudes",
    )(*(pltpu.with_memory_space_constraint(block.reshape(2048, 128), pltpu.HBM) for block in (t_own, t_oth)))


def ladder_kernel(place, right, *refs):
    own, oth, (t_high_in, t_low_in, out) = refs[:8], refs[8:11], refs[11:14]
    r_buf, raw, parts, t_high, t_low, acc, y_high, y_low, flip, r_sem, l_sem, t_sem = refs[14:]
    swapped = {slot: ref.at[i] for group, ref in zip(GROUPS, oth) for i, slot in enumerate(group)}
    y, sign, xl_here, xh, core = (place[i] for i in range(5))

    def pair(k):
        return lax.rem(y // 2 + PAIRS[k], 4)

    def right_copy(k, order):
        where = lax.bitwise_xor(order, xl_here) * 4 + pair(k)
        return pltpu.make_async_copy(right.at[where], r_buf.at[k, order], r_sem.at[k, order])

    def left_copy(side, slot):
        return pltpu.make_async_copy(swapped[slot] if side else own[slot], raw.at[side, slot], l_sem.at[side, slot])

    def left(k, q_half, half, order):
        at = 2 * pair(k) + lax.bitwise_xor(half, xh)
        steps = (y - at) * sign
        side = lax.bitwise_xor(core, q_half)
        slot = lax.bitwise_and(8 + steps - 2 * side * steps, 7)
        return parts[side, slot, order]

    t_copies = [
        pltpu.make_async_copy(t_high_in, t_high, t_sem.at[0]),
        pltpu.make_async_copy(t_low_in, t_low, t_sem.at[1]),
    ]
    for k in range(4):
        for slot in NEEDED[k]:
            for side in range(2):
                left_copy(side, slot).start()
        for order in range(2):
            right_copy(k, order).start()
    for copy in t_copies:
        copy.start()
    for k in range(4):
        for slot in NEEDED[k]:
            for side in range(2):
                left_copy(side, slot).wait()
                high, low = split(raw[side, slot])
                parts[side, slot, :, :, :, :128] = high
                parts[side, slot, :, :, :, 128:] = low
        for order in range(2):
            right_copy(k, order).wait()
        r_high, r_low, l_high, l_low = [], [], [], []
        for order in range(2):
            high, low = split(r_buf[k, order].reshape(512, 256))
            r_high.append(high)
            r_low.append(low)
            for q_half in range(2):
                both = jnp.concatenate([left(k, q_half, half, order) for half in range(2)], axis=1).reshape(1024, 256)
                l_high.append(both[:, :128])
                l_low.append(both[:, 128:])
        product = dot_nt(
            jnp.concatenate(r_high + r_low + r_high, axis=1),
            jnp.concatenate(l_high + l_high + l_low, axis=1),
        )
        for a in range(8):
            piece = product[:, a * 128 : a * 128 + 128]
            if k == 0:
                acc[a] = piece
            else:
                acc[a] += piece
    for copy in t_copies:
        copy.wait()
    for d in range(32):
        for a in range(8):
            high, low = split(acc[a, pl.ds(d, 16, 32), :])
            y_high[a * 16 : a * 16 + 16, d * 128 : d * 128 + 128] = high
            y_low[a * 16 : a * 16 + 16, d * 128 : d * 128 + 128] = low
    total = dot_nn(y_high[...], t_high[...]) + dot_nn(y_high[...], t_low[...]) + dot_nn(y_low[...], t_high[...])
    for a in range(8):
        flip[pl.ds(a, 16, 8), :] = total[a * 16 : a * 16 + 16]
    total = flip[...].T
    for xl in range(2):
        for each in range(2):
            for row in range(8):
                first = xl * 64 + row * 8 + each * 4
                for xh_to in range(2):
                    out[xh_to * 4 + xl * 2 + each, row * 4 : row * 4 + 4] = total[first : first + 4]


def contract(place, right, own, oth, t_split):
    return pl.pallas_call(
        ladder_kernel,
        out_shape=jax.ShapeDtypeStruct((8, 32, 128), jnp.float32),
        in_specs=[pl.BlockSpec(memory_space=pltpu.SMEM)] + [pl.BlockSpec(memory_space=pl.ANY)] * 14,
        out_specs=pl.BlockSpec(memory_space=pltpu.VMEM),
        scratch_shapes=[
            pltpu.VMEM((4, 2, 16, 32, 256), jnp.float32),
            pltpu.VMEM((2, 8, 2, 8, 64, 128), jnp.float32),
            pltpu.VMEM((2, 8, 2, 8, 64, 256), jnp.bfloat16),
            pltpu.VMEM((4096, 128), jnp.bfloat16),
            pltpu.VMEM((4096, 128), jnp.bfloat16),
            pltpu.VMEM((8, 512, 128), jnp.float32),
            pltpu.VMEM((128, 4096), jnp.bfloat16),
            pltpu.VMEM((128, 4096), jnp.bfloat16),
            pltpu.VMEM((128, 128), jnp.float32),
            pltpu.SemaphoreType.DMA((4, 2)),
            pltpu.SemaphoreType.DMA((2, 8)),
            pltpu.SemaphoreType.DMA((2,)),
        ],
        compiler_params=pltpu.CompilerParams(vmem_limit_bytes=60 * 1024 * 1024),
        cost_estimate=pl.CostEstimate(flops=6 << 30, bytes_accessed=16 << 20, transcendentals=0),
        name="ladder",
    )(place, right, *own, *oth, *t_split)


def pack_kernel(near, out, total):
    value = near[0]
    for part in range(1, 8):
        value += near[part]
    total[...] = value
    lane = lax.broadcasted_iota(jnp.int32, (8, 128), 1) // 16
    for z in range(8):
        packed = jnp.zeros((8, 128), jnp.float32)
        for k in range(4):
            rows = total[pl.ds(k, 8, 4), :]
            shift = (k - z) * 16 % 128
            packed = jnp.where(lane == k, pltpu.roll(rows, shift, 1) if shift else rows, packed)
        out[z * 8 : z * 8 + 8, :] = packed


def pack(near):
    return pl.pallas_call(
        pack_kernel,
        out_shape=jax.ShapeDtypeStruct((64, 128), jnp.float32),
        scratch_shapes=[pltpu.VMEM((32, 128), jnp.float32)],
        name="pack",
    )(near)


def hold_kernel(place, piece, out):
    for i in range(5):
        out[i] = place[i]


def hold(place, piece):
    smem = pl.BlockSpec(memory_space=pltpu.SMEM)
    return pl.pallas_call(
        hold_kernel,
        out_shape=jax.ShapeDtypeStruct((5,), jnp.int32),
        in_specs=[smem, pl.BlockSpec(memory_space=pl.ANY)],
        out_specs=smem,
        cost_estimate=pl.CostEstimate(flops=30 << 30, bytes_accessed=1 << 10, transcendentals=0),
        name="hold",
    )(place, piece)


def shards(vectors_left, vectors_right, amplitudes):
    xh, y, core = (lax.axis_index(name) for name in ("xh", "y", "core"))
    place = jnp.stack([y, 1 - 2 * core, lax.axis_index("xl"), xh, core]).astype(jnp.int32)
    right = lax.all_gather(vectors_right, "z", axis=0)
    own = jnp.stack([send(vectors_left, SAME_XL), send(vectors_left, OTHER_XL)])
    x1 = send(own, RING_X)
    t_oth = send(amplitudes, SWAP_XH)
    y1 = send(own, RING_Y)
    x2 = send(x1, RING_X)
    y2 = send(after(y1, x1), RING_Y)
    x3 = send(after(x2, y1), RING_X)
    y3 = send(after(y2, x2), RING_Y)
    x4 = send(after(x3, y2), RING_X)
    t_split = split_amplitudes(amplitudes, t_oth)
    left_own = [own, x1, x2, x3, x4, y3, y2, y1]
    gates = ((x3, t_oth), t_split, ())
    left_oth = [
        send(after(jnp.stack([left_own[slot] for slot in group]), *gate), SWAP_CORE) for group, gate in zip(GROUPS, gates)
    ]
    partial = contract(hold(place, x4), right, left_own, left_oth, t_split)
    near = pack(lax.all_to_all(partial, ("xh", "xl", "core"), 0, 0, tiled=True))
    far = jnp.sum(lax.all_to_all(near, ("z", "y"), 0, 0, tiled=True), axis=0)
    return lax.dynamic_slice(far[:64].reshape(4, 2, 8), (0, xh, 0), (4, 1, 8)).reshape(4, 8, 1)


def solution(mesh):
    fine = Mesh(mesh.devices.reshape(SIZES), AXES)
    c_axes, d_axes = ("z", "xh"), ("xl", "y", "core")
    return jax.shard_map(
        shards,
        mesh=fine,
        in_specs=(P(None, c_axes, d_axes), P(None, d_axes, c_axes), P(c_axes, d_axes, None)),
        out_specs=P(d_axes, None, c_axes),
        check_vma=False,
    )
```

```python
import jax
import jax.numpy as jnp
from jax import lax
from jax.experimental import pallas as pl
from jax.experimental.pallas import tpu as pltpu
from jax.sharding import Mesh, PartitionSpec as P

AXES = ("z", "xh", "xl", "y", "core")
SIZES = (8, 2, 2, 8, 2)


def linear(z, xh, xl, y, core):
    return (((z % 8) * 2 + xh) * 2 + xl) * 16 + (y % 8) * 2 + core


def table(target):
    pairs = []
    for z in range(8):
        for xh in range(2):
            for xl in range(2):
                for y in range(8):
                    for core in range(2):
                        pairs.append((linear(z, xh, xl, y, core), linear(*target(z, xh, xl, y, core))))
    return pairs


SAME_XL = table(lambda z, xh, xl, y, core: (z, y % 2, xl, y // 2 * 2 + xh, core))
OTHER_XL = table(lambda z, xh, xl, y, core: (z, y % 2, 1 - xl, y // 2 * 2 + xh, core))
RING_X = table(lambda z, xh, xl, y, core: (z, xh, xl, y + 1 - 2 * core, core))
RING_Y = table(lambda z, xh, xl, y, core: (z, xh, xl, y - 1 + 2 * core, core))
SWAP_CORE = table(lambda z, xh, xl, y, core: (z, xh, xl, y, 1 - core))
SWAP_XH = table(lambda z, xh, xl, y, core: (z, 1 - xh, xl, y, core))
PAIRS = (0, 1, 3, 2)
NEEDED = ((0, 1, 7), (2, 6, 3, 5), (4,), ())


def send(array, pairs):
    return lax.ppermute(array, AXES, pairs)


def after(array, *earlier):
    return lax.optimization_barrier((array, *earlier))[0]


def split(value):
    high = value.astype(jnp.bfloat16)
    low = (value - high.astype(jnp.float32)).astype(jnp.bfloat16)
    return high, low


def dot_nt(a, b):
    return lax.dot_general(a, b, (((1,), (1,)), ((), ())), preferred_element_type=jnp.float32)


def dot_nn(a, b):
    return lax.dot_general(a, b, (((1,), (0,)), ((), ())), preferred_element_type=jnp.float32)


def amplitudes_kernel(block, out, raw, parts, sems):
    copy = pltpu.make_async_copy(block, raw, sems.at[0])
    copy.start()
    copy.wait()
    for d in range(32):
        high, low = split(raw[pl.ds(d, 64, 32), :])
        parts[0, d] = high
        parts[1, d] = low
    copy = pltpu.make_async_copy(parts, out, sems.at[1])
    copy.start()
    copy.wait()


def split_amplitudes(block):
    return pl.pallas_call(
        amplitudes_kernel,
        out_shape=pltpu.HBM((2, 32, 64, 128), jnp.bfloat16),
        in_specs=[pl.BlockSpec(memory_space=pl.ANY)],
        out_specs=pl.BlockSpec(memory_space=pltpu.HBM),
        scratch_shapes=[
            pltpu.VMEM((2048, 128), jnp.float32),
            pltpu.VMEM((2, 32, 64, 128), jnp.bfloat16),
            pltpu.SemaphoreType.DMA((2,)),
        ],
        compiler_params=pltpu.CompilerParams(vmem_limit_bytes=8 * 1024 * 1024),
        cost_estimate=pl.CostEstimate(flops=1 << 20, bytes_accessed=2 << 20, transcendentals=0),
        name="split_amplitudes",
    )(pltpu.with_memory_space_constraint(block.reshape(2048, 128), pltpu.HBM))


def ladder_kernel(place, right, *refs):
    pieces, (t_own, t_oth, out) = (refs[:8], refs[8:16]), refs[16:19]
    r_buf, raw, parts, t_buf, acc, y_high, y_low, flip, r_sem, l_sem, t_sem = refs[19:]
    y, sign, xl_here, xh, core = (place[i] for i in range(5))

    def pair(k):
        return lax.rem(y // 2 + PAIRS[k], 4)

    def right_copy(k, order):
        where = lax.bitwise_xor(order, xl_here) * 4 + pair(k)
        return pltpu.make_async_copy(right.at[where], r_buf.at[k, order], r_sem.at[k, order])

    def left_copy(side, slot):
        return pltpu.make_async_copy(pieces[side][slot], raw.at[side, slot], l_sem.at[side, slot])

    def left(k, q_half, half, order):
        at = 2 * pair(k) + lax.bitwise_xor(half, xh)
        steps = (y - at) * sign
        side = lax.bitwise_xor(core, q_half)
        slot = lax.bitwise_and(8 + steps - 2 * side * steps, 7)
        return parts[side, slot, order]

    t_copies = [
        pltpu.make_async_copy(ref, t_buf.at[:, :, half], t_sem.at[half]) for half, ref in enumerate((t_own, t_oth))
    ]
    for k in range(4):
        for slot in NEEDED[k]:
            for side in range(2):
                left_copy(side, slot).start()
        for order in range(2):
            right_copy(k, order).start()
    for copy in t_copies:
        copy.start()
    for k in range(4):
        for slot in NEEDED[k]:
            for side in range(2):
                left_copy(side, slot).wait()
                high, low = split(raw[side, slot])
                parts[side, slot, :, :, :, :128] = high
                parts[side, slot, :, :, :, 128:] = low
        for order in range(2):
            right_copy(k, order).wait()
        r_high, r_low, l_high, l_low = [], [], [], []
        for order in range(2):
            high, low = split(r_buf[k, order].reshape(512, 256))
            r_high.append(high)
            r_low.append(low)
            for q_half in range(2):
                both = jnp.concatenate([left(k, q_half, half, order) for half in range(2)], axis=1).reshape(1024, 256)
                l_high.append(both[:, :128])
                l_low.append(both[:, 128:])
        product = dot_nt(
            jnp.concatenate(r_high + r_low + r_high, axis=1),
            jnp.concatenate(l_high + l_high + l_low, axis=1),
        )
        for a in range(8):
            piece = product[:, a * 128 : a * 128 + 128]
            if k == 0:
                acc[a] = piece
            else:
                acc[a] += piece
    for copy in t_copies:
        copy.wait()
    for d in range(32):
        for a in range(8):
            high, low = split(acc[a, pl.ds(d, 16, 32), :])
            y_high[a * 16 : a * 16 + 16, d * 128 : d * 128 + 128] = high
            y_low[a * 16 : a * 16 + 16, d * 128 : d * 128 + 128] = low
    t_high, t_low = (t_buf[i].reshape(4096, 128) for i in range(2))
    total = dot_nn(y_high[...], t_high) + dot_nn(y_high[...], t_low) + dot_nn(y_low[...], t_high)
    for a in range(8):
        flip[pl.ds(a, 16, 8), :] = total[a * 16 : a * 16 + 16]
    total = flip[...].T
    for xl in range(2):
        for each in range(2):
            for row in range(8):
                first = xl * 64 + row * 8 + each * 4
                for xh_to in range(2):
                    out[xh_to * 4 + xl * 2 + each, row * 4 : row * 4 + 4] = total[first : first + 4]


def contract(place, right, own, oth, t_split):
    return pl.pallas_call(
        ladder_kernel,
        out_shape=jax.ShapeDtypeStruct((8, 32, 128), jnp.float32),
        in_specs=[pl.BlockSpec(memory_space=pltpu.SMEM)] + [pl.BlockSpec(memory_space=pl.ANY)] * 19,
        out_specs=pl.BlockSpec(memory_space=pltpu.VMEM),
        scratch_shapes=[
            pltpu.VMEM((4, 2, 16, 32, 256), jnp.float32),
            pltpu.VMEM((2, 8, 2, 8, 64, 128), jnp.float32),
            pltpu.VMEM((2, 8, 2, 8, 64, 256), jnp.bfloat16),
            pltpu.VMEM((2, 32, 2, 64, 128), jnp.bfloat16),
            pltpu.VMEM((8, 512, 128), jnp.float32),
            pltpu.VMEM((128, 4096), jnp.bfloat16),
            pltpu.VMEM((128, 4096), jnp.bfloat16),
            pltpu.VMEM((128, 128), jnp.float32),
            pltpu.SemaphoreType.DMA((4, 2)),
            pltpu.SemaphoreType.DMA((2, 8)),
            pltpu.SemaphoreType.DMA((2,)),
        ],
        compiler_params=pltpu.CompilerParams(vmem_limit_bytes=60 * 1024 * 1024),
        cost_estimate=pl.CostEstimate(flops=6 << 30, bytes_accessed=16 << 20, transcendentals=0),
        name="ladder",
    )(place, right, *own, *oth, *t_split)


def pack_kernel(near, out, total):
    value = near[0]
    for part in range(1, 8):
        value += near[part]
    total[...] = value
    lane = lax.broadcasted_iota(jnp.int32, (8, 128), 1) // 16
    for z in range(8):
        packed = jnp.zeros((8, 128), jnp.float32)
        for k in range(4):
            rows = total[pl.ds(k, 8, 4), :]
            shift = (k - z) * 16 % 128
            packed = jnp.where(lane == k, pltpu.roll(rows, shift, 1) if shift else rows, packed)
        out[z * 8 : z * 8 + 8, :] = packed


def pack(near):
    return pl.pallas_call(
        pack_kernel,
        out_shape=jax.ShapeDtypeStruct((64, 128), jnp.float32),
        scratch_shapes=[pltpu.VMEM((32, 128), jnp.float32)],
        name="pack",
    )(near)


def shards(vectors_left, vectors_right, amplitudes):
    xh, y, core = (lax.axis_index(name) for name in ("xh", "y", "core"))
    place = jnp.stack([y, 1 - 2 * core, lax.axis_index("xl"), xh, core]).astype(jnp.int32)
    right = lax.all_gather(vectors_right, "z", axis=0)
    t_own_split = split_amplitudes(amplitudes)
    same, other = send(vectors_left, SAME_XL), send(vectors_left, OTHER_XL)
    own = jnp.stack([after(same, t_own_split), other])
    x1 = send(own, RING_X)
    t_oth = send(amplitudes, SWAP_XH)
    y1 = send(own, RING_Y)
    own_swapped = send(own, SWAP_CORE)
    x2 = send(x1, RING_X)
    y2 = send(after(y1, x1), RING_Y)
    x1_swapped = send(after(x1, own_swapped), SWAP_CORE)
    x3 = send(after(x2, y1), RING_X)
    y3 = send(after(y2, x2), RING_Y)
    x4 = send(after(x3, y2, t_oth), RING_X)
    t_split = (t_own_split, split_amplitudes(after(t_oth, x4)))
    left_own = [own, x1, x2, x3, x4, y3, y2, y1]
    left_oth = [own_swapped, x1_swapped] + [send(piece, SWAP_CORE) for piece in left_own[2:]]
    partial = contract(place, right, left_own, left_oth, t_split)
    near = pack(lax.all_to_all(partial, ("xh", "xl", "core"), 0, 0, tiled=True))
    far = jnp.sum(lax.all_to_all(near, ("z", "y"), 0, 0, tiled=True), axis=0)
    return lax.dynamic_slice(far[:64].reshape(4, 2, 8), (0, xh, 0), (4, 1, 8)).reshape(4, 8, 1)


def solution(mesh):
    fine = Mesh(mesh.devices.reshape(SIZES), AXES)
    c_axes, d_axes = ("z", "xh"), ("xl", "y", "core")
    return jax.shard_map(
        shards,
        mesh=fine,
        in_specs=(P(None, c_axes, d_axes), P(None, d_axes, c_axes), P(c_axes, d_axes, None)),
        out_specs=P(d_axes, None, c_axes),
        check_vma=False,
    )
```

```python
import jax
import jax.numpy as jnp
from jax import lax
from jax.experimental import pallas as pl
from jax.experimental.pallas import tpu as pltpu
from jax.sharding import Mesh, PartitionSpec as P

AXES = ("z", "xh", "xl", "y", "core")
SIZES = (8, 2, 2, 8, 2)


def linear(z, xh, xl, y, core):
    return (((z % 8) * 2 + xh) * 2 + xl) * 16 + (y % 8) * 2 + core


def table(target):
    pairs = []
    for z in range(8):
        for xh in range(2):
            for xl in range(2):
                for y in range(8):
                    for core in range(2):
                        pairs.append((linear(z, xh, xl, y, core), linear(*target(z, xh, xl, y, core))))
    return pairs


SAME_XL = table(lambda z, xh, xl, y, core: (z, y % 2, xl, y // 2 * 2 + xh, core))
OTHER_XL = table(lambda z, xh, xl, y, core: (z, y % 2, 1 - xl, y // 2 * 2 + xh, core))
RING_X = table(lambda z, xh, xl, y, core: (z, xh, xl, y + 1 - 2 * core, core))
RING_Y = table(lambda z, xh, xl, y, core: (z, xh, xl, y - 1 + 2 * core, core))
SWAP_CORE = table(lambda z, xh, xl, y, core: (z, xh, xl, y, 1 - core))
SWAP_XH = table(lambda z, xh, xl, y, core: (z, 1 - xh, xl, y, core))
PAIRS = (0, 1, 3, 2)
NEEDED = ((0, 1, 7), (2, 6, 3, 5), (4,), ())


def send(array, pairs):
    return lax.ppermute(array, AXES, pairs)


def after(array, *earlier):
    return lax.optimization_barrier((array, *earlier))[0]


def split(value):
    high = value.astype(jnp.bfloat16)
    low = (value - high.astype(jnp.float32)).astype(jnp.bfloat16)
    return high, low


def dot_nt(a, b):
    return lax.dot_general(a, b, (((1,), (1,)), ((), ())), preferred_element_type=jnp.float32)


def dot_nn(a, b):
    return lax.dot_general(a, b, (((1,), (0,)), ((), ())), preferred_element_type=jnp.float32)


def amplitudes_kernel(block, out, raw, parts, sems):
    copy = pltpu.make_async_copy(block, raw, sems.at[0])
    copy.start()
    copy.wait()
    for d in range(32):
        high, low = split(raw[pl.ds(d, 64, 32), :])
        parts[0, d] = high
        parts[1, d] = low
    copy = pltpu.make_async_copy(parts, out, sems.at[1])
    copy.start()
    copy.wait()


def split_amplitudes(block):
    return pl.pallas_call(
        amplitudes_kernel,
        out_shape=pltpu.HBM((2, 32, 64, 128), jnp.bfloat16),
        in_specs=[pl.BlockSpec(memory_space=pl.ANY)],
        out_specs=pl.BlockSpec(memory_space=pltpu.HBM),
        scratch_shapes=[
            pltpu.VMEM((2048, 128), jnp.float32),
            pltpu.VMEM((2, 32, 64, 128), jnp.bfloat16),
            pltpu.SemaphoreType.DMA((2,)),
        ],
        compiler_params=pltpu.CompilerParams(vmem_limit_bytes=8 * 1024 * 1024),
        cost_estimate=pl.CostEstimate(flops=1 << 20, bytes_accessed=2 << 20, transcendentals=0),
        name="split_amplitudes",
    )(pltpu.with_memory_space_constraint(block.reshape(2048, 128), pltpu.HBM))


def ladder_kernel(place, right, *refs):
    pieces, (t_own, t_oth, out) = (refs[:8], refs[8:16]), refs[16:19]
    r_buf, raw, parts, t_buf, acc, y_high, y_low, flip, r_sem, l_sem, t_sem = refs[19:]
    y, sign, xl_here, xh, core = (place[i] for i in range(5))

    def pair(k):
        return lax.rem(y // 2 + PAIRS[k], 4)

    def right_copy(k, order):
        where = lax.bitwise_xor(order, xl_here) * 4 + pair(k)
        return pltpu.make_async_copy(right.at[where], r_buf.at[k, order], r_sem.at[k, order])

    def left_copy(side, slot):
        return pltpu.make_async_copy(pieces[side][slot], raw.at[side, slot], l_sem.at[side, slot])

    def left(k, q_half, half, order):
        at = 2 * pair(k) + lax.bitwise_xor(half, xh)
        steps = (y - at) * sign
        side = lax.bitwise_xor(core, q_half)
        slot = lax.bitwise_and(8 + steps - 2 * side * steps, 7)
        return parts[side, slot, order]

    t_copies = [
        pltpu.make_async_copy(ref, t_buf.at[:, :, half], t_sem.at[half]) for half, ref in enumerate((t_own, t_oth))
    ]
    for k in range(4):
        for slot in NEEDED[k]:
            for side in range(2):
                left_copy(side, slot).start()
        for order in range(2):
            right_copy(k, order).start()
    for copy in t_copies:
        copy.start()
    for k in range(4):
        for slot in NEEDED[k]:
            for side in range(2):
                left_copy(side, slot).wait()
                high, low = split(raw[side, slot])
                parts[side, slot, :, :, :, :128] = high
                parts[side, slot, :, :, :, 128:] = low
        for order in range(2):
            right_copy(k, order).wait()
        r_high, r_low, l_high, l_low = [], [], [], []
        for order in range(2):
            high, low = split(r_buf[k, order].reshape(512, 256))
            r_high.append(high)
            r_low.append(low)
            for q_half in range(2):
                both = jnp.concatenate([left(k, q_half, half, order) for half in range(2)], axis=1).reshape(1024, 256)
                l_high.append(both[:, :128])
                l_low.append(both[:, 128:])
        product = dot_nt(
            jnp.concatenate(r_high + r_low + r_high, axis=1),
            jnp.concatenate(l_high + l_high + l_low, axis=1),
        )
        for a in range(8):
            piece = product[:, a * 128 : a * 128 + 128]
            if k == 0:
                acc[a] = piece
            else:
                acc[a] += piece
    for copy in t_copies:
        copy.wait()
    for d in range(32):
        for a in range(8):
            high, low = split(acc[a, pl.ds(d, 16, 32), :])
            y_high[a * 16 : a * 16 + 16, d * 128 : d * 128 + 128] = high
            y_low[a * 16 : a * 16 + 16, d * 128 : d * 128 + 128] = low
    t_high, t_low = (t_buf[i].reshape(4096, 128) for i in range(2))
    total = dot_nn(y_high[...], t_high) + dot_nn(y_high[...], t_low) + dot_nn(y_low[...], t_high)
    for a in range(8):
        flip[pl.ds(a, 16, 8), :] = total[a * 16 : a * 16 + 16]
    total = flip[...].T
    for xh_to in range(2):
        out[xh_to] = total


def contract(place, right, own, oth, t_split):
    return pl.pallas_call(
        ladder_kernel,
        out_shape=jax.ShapeDtypeStruct((2, 128, 128), jnp.float32),
        in_specs=[pl.BlockSpec(memory_space=pltpu.SMEM)] + [pl.BlockSpec(memory_space=pl.ANY)] * 19,
        out_specs=pl.BlockSpec(memory_space=pltpu.VMEM),
        scratch_shapes=[
            pltpu.VMEM((4, 2, 16, 32, 256), jnp.float32),
            pltpu.VMEM((2, 8, 2, 8, 64, 128), jnp.float32),
            pltpu.VMEM((2, 8, 2, 8, 64, 256), jnp.bfloat16),
            pltpu.VMEM((2, 32, 2, 64, 128), jnp.bfloat16),
            pltpu.VMEM((8, 512, 128), jnp.float32),
            pltpu.VMEM((128, 4096), jnp.bfloat16),
            pltpu.VMEM((128, 4096), jnp.bfloat16),
            pltpu.VMEM((128, 128), jnp.float32),
            pltpu.SemaphoreType.DMA((4, 2)),
            pltpu.SemaphoreType.DMA((2, 8)),
            pltpu.SemaphoreType.DMA((2,)),
        ],
        compiler_params=pltpu.CompilerParams(vmem_limit_bytes=60 * 1024 * 1024),
        cost_estimate=pl.CostEstimate(flops=6 << 30, bytes_accessed=16 << 20, transcendentals=0),
        name="ladder",
    )(place, right, *own, *oth, *t_split)


def shards(vectors_left, vectors_right, amplitudes):
    z, xh, y, core = (lax.axis_index(name) for name in ("z", "xh", "y", "core"))
    place = jnp.stack([y, 1 - 2 * core, lax.axis_index("xl"), xh, core]).astype(jnp.int32)
    right = lax.all_gather(vectors_right, "z", axis=0)
    t_own_split = split_amplitudes(amplitudes)
    same, other = send(vectors_left, SAME_XL), send(vectors_left, OTHER_XL)
    own = jnp.stack([after(same, t_own_split), other])
    x1 = send(own, RING_X)
    t_oth = send(amplitudes, SWAP_XH)
    y1 = send(own, RING_Y)
    own_swapped = send(own, SWAP_CORE)
    x2 = send(x1, RING_X)
    y2 = send(after(y1, x1), RING_Y)
    x1_swapped = send(after(x1, own_swapped), SWAP_CORE)
    x3 = send(after(x2, y1), RING_X)
    y3 = send(after(y2, x2), RING_Y)
    x4 = send(after(x3, y2, t_oth), RING_X)
    t_split = (t_own_split, split_amplitudes(after(t_oth, x4)))
    left_own = [own, x1, x2, x3, x4, y3, y2, y1]
    left_oth = [own_swapped, x1_swapped] + [send(piece, SWAP_CORE) for piece in left_own[2:]]
    partial = contract(place, right, left_own, left_oth, t_split)
    near = lax.all_to_all(partial.reshape(64, 4, 128), ("xh", "xl", "y", "core"), 0, 0, tiled=True)
    near = jnp.broadcast_to(jnp.sum(near, axis=0), (8, 4, 128))
    far = jnp.sum(lax.all_to_all(near, "z", 0, 0, tiled=True), axis=0)
    return lax.dynamic_slice(far.reshape(4, 16, 8), (0, z * 2 + xh, 0), (4, 1, 8)).reshape(4, 8, 1)


def solution(mesh):
    fine = Mesh(mesh.devices.reshape(SIZES), AXES)
    c_axes, d_axes = ("z", "xh"), ("xl", "y", "core")
    return jax.shard_map(
        shards,
        mesh=fine,
        in_specs=(P(None, c_axes, d_axes), P(None, d_axes, c_axes), P(c_axes, d_axes, None)),
        out_specs=P(d_axes, None, c_axes),
        check_vma=False,
    )
```

```python
import jax
import jax.numpy as jnp
from jax import lax
from jax.experimental import pallas as pl
from jax.experimental.pallas import tpu as pltpu
from jax.sharding import Mesh, PartitionSpec as P

AXES = ("z", "xh", "xl", "y", "core")
SIZES = (8, 2, 2, 8, 2)


def linear(z, xh, xl, y, core):
    return (((z % 8) * 2 + xh) * 2 + xl) * 16 + (y % 8) * 2 + core


def table(target):
    pairs = []
    for z in range(8):
        for xh in range(2):
            for xl in range(2):
                for y in range(8):
                    for core in range(2):
                        pairs.append((linear(z, xh, xl, y, core), linear(*target(z, xh, xl, y, core))))
    return pairs


SAME_XL = table(lambda z, xh, xl, y, core: (z, y % 2, xl, y // 2 * 2 + xh, core))
OTHER_XL = table(lambda z, xh, xl, y, core: (z, y % 2, 1 - xl, y // 2 * 2 + xh, core))
RING_X = table(lambda z, xh, xl, y, core: (z, xh, xl, y + 1 - 2 * core, core))
RING_Y = table(lambda z, xh, xl, y, core: (z, xh, xl, y - 1 + 2 * core, core))
SWAP_CORE = table(lambda z, xh, xl, y, core: (z, xh, xl, y, 1 - core))
SWAP_XH = table(lambda z, xh, xl, y, core: (z, 1 - xh, xl, y, core))
PAIRS = (0, 1, 3, 2)
NEEDED = ((0, 1, 7), (2, 6, 3, 5), (4,), ())


def send(array, pairs):
    return lax.ppermute(array, AXES, pairs)


def after(array, *earlier):
    return lax.optimization_barrier((array, *earlier))[0]


def split(value):
    high = value.astype(jnp.bfloat16)
    low = (value - high.astype(jnp.float32)).astype(jnp.bfloat16)
    return high, low


def dot_nt(a, b):
    return lax.dot_general(a, b, (((1,), (1,)), ((), ())), preferred_element_type=jnp.float32)


def dot_nn(a, b):
    return lax.dot_general(a, b, (((1,), (0,)), ((), ())), preferred_element_type=jnp.float32)


def amplitudes_kernel(block, out, raw, parts, sems):
    copy = pltpu.make_async_copy(block, raw, sems.at[0])
    copy.start()
    copy.wait()
    for d in range(32):
        high, low = split(raw[pl.ds(d, 64, 32), :])
        parts[0, d] = high
        parts[1, d] = low
    copy = pltpu.make_async_copy(parts, out, sems.at[1])
    copy.start()
    copy.wait()


def split_amplitudes(block):
    return pl.pallas_call(
        amplitudes_kernel,
        out_shape=pltpu.HBM((2, 32, 64, 128), jnp.bfloat16),
        in_specs=[pl.BlockSpec(memory_space=pl.ANY)],
        out_specs=pl.BlockSpec(memory_space=pltpu.HBM),
        scratch_shapes=[
            pltpu.VMEM((2048, 128), jnp.float32),
            pltpu.VMEM((2, 32, 64, 128), jnp.bfloat16),
            pltpu.SemaphoreType.DMA((2,)),
        ],
        compiler_params=pltpu.CompilerParams(vmem_limit_bytes=8 * 1024 * 1024),
        cost_estimate=pl.CostEstimate(flops=1 << 20, bytes_accessed=2 << 20, transcendentals=0),
        name="split_amplitudes",
    )(pltpu.with_memory_space_constraint(block.reshape(2048, 128), pltpu.HBM))


def ladder_kernel(place, right, *refs):
    pieces, (t_own, t_oth, out) = (refs[:8], refs[8:16]), refs[16:19]
    r_buf, raw, parts, t_buf, acc, y_high, y_low, flip, rows, r_sem, l_sem, t_sem = refs[19:]
    y, sign, xl_here, xh, core = (place[i] for i in range(5))

    def pair(k):
        return lax.rem(y // 2 + PAIRS[k], 4)

    def right_copy(k, order):
        where = lax.bitwise_xor(order, xl_here) * 4 + pair(k)
        return pltpu.make_async_copy(right.at[where], r_buf.at[k, order], r_sem.at[k, order])

    def left_copy(side, slot):
        return pltpu.make_async_copy(pieces[side][slot], raw.at[side, slot], l_sem.at[side, slot])

    def left(k, q_half, half, order):
        at = 2 * pair(k) + lax.bitwise_xor(half, xh)
        steps = (y - at) * sign
        side = lax.bitwise_xor(core, q_half)
        slot = lax.bitwise_and(8 + steps - 2 * side * steps, 7)
        return parts[side, slot, order]

    t_copies = [
        pltpu.make_async_copy(ref, t_buf.at[:, :, half], t_sem.at[half]) for half, ref in enumerate((t_own, t_oth))
    ]
    for k in range(4):
        for slot in NEEDED[k]:
            for side in range(2):
                left_copy(side, slot).start()
        for order in range(2):
            right_copy(k, order).start()
    for copy in t_copies:
        copy.start()
    for k in range(4):
        for slot in NEEDED[k]:
            for side in range(2):
                left_copy(side, slot).wait()
                high, low = split(raw[side, slot])
                parts[side, slot, :, :, :, :128] = high
                parts[side, slot, :, :, :, 128:] = low
        for order in range(2):
            right_copy(k, order).wait()
        r_high, r_low, l_high, l_low = [], [], [], []
        for order in range(2):
            high, low = split(r_buf[k, order].reshape(512, 256))
            r_high.append(high)
            r_low.append(low)
            for q_half in range(2):
                both = jnp.concatenate([left(k, q_half, half, order) for half in range(2)], axis=1).reshape(1024, 256)
                l_high.append(both[:, :128])
                l_low.append(both[:, 128:])
        product = dot_nt(
            jnp.concatenate(r_high + r_low + r_high, axis=1),
            jnp.concatenate(l_high + l_high + l_low, axis=1),
        )
        for a in range(8):
            piece = product[:, a * 128 : a * 128 + 128]
            if k == 0:
                acc[a] = piece
            else:
                acc[a] += piece
    for copy in t_copies:
        copy.wait()
    for d in range(32):
        for a in range(8):
            high, low = split(acc[a, pl.ds(d, 16, 32), :])
            y_high[a * 16 : a * 16 + 16, d * 128 : d * 128 + 128] = high
            y_low[a * 16 : a * 16 + 16, d * 128 : d * 128 + 128] = low
    t_high, t_low = (t_buf[i].reshape(4096, 128) for i in range(2))
    total = dot_nn(y_high[...], t_high) + dot_nn(y_high[...], t_low) + dot_nn(y_low[...], t_high)
    rows[...] = total
    for a in range(8):
        for xh_to in range(2):
            flip[pl.ds(xh_to * 64 + a, 8, 8), :] = rows[pl.ds(a * 16 + xh_to, 8, 2), :]
    rows[...] = flip[...].T
    even, odd = rows[pl.ds(0, 64, 2), :], rows[pl.ds(1, 64, 2), :]
    left_half = lax.broadcasted_iota(jnp.int32, (64, 128), 1) < 64
    out[0] = jnp.where(left_half, even, pltpu.roll(odd, 64, 1))
    out[1] = jnp.where(left_half, pltpu.roll(even, 64, 1), odd)


def contract(place, right, own, oth, t_split):
    return pl.pallas_call(
        ladder_kernel,
        out_shape=jax.ShapeDtypeStruct((2, 64, 128), jnp.float32),
        in_specs=[pl.BlockSpec(memory_space=pltpu.SMEM)] + [pl.BlockSpec(memory_space=pl.ANY)] * 19,
        out_specs=pl.BlockSpec(memory_space=pltpu.VMEM),
        scratch_shapes=[
            pltpu.VMEM((4, 2, 16, 32, 256), jnp.float32),
            pltpu.VMEM((2, 8, 2, 8, 64, 128), jnp.float32),
            pltpu.VMEM((2, 8, 2, 8, 64, 256), jnp.bfloat16),
            pltpu.VMEM((2, 32, 2, 64, 128), jnp.bfloat16),
            pltpu.VMEM((8, 512, 128), jnp.float32),
            pltpu.VMEM((128, 4096), jnp.bfloat16),
            pltpu.VMEM((128, 4096), jnp.bfloat16),
            pltpu.VMEM((128, 128), jnp.float32),
            pltpu.VMEM((128, 128), jnp.float32),
            pltpu.SemaphoreType.DMA((4, 2)),
            pltpu.SemaphoreType.DMA((2, 8)),
            pltpu.SemaphoreType.DMA((2,)),
        ],
        compiler_params=pltpu.CompilerParams(vmem_limit_bytes=60 * 1024 * 1024),
        cost_estimate=pl.CostEstimate(flops=6 << 30, bytes_accessed=16 << 20, transcendentals=0),
        name="ladder",
    )(place, right, *own, *oth, *t_split)


def shards(vectors_left, vectors_right, amplitudes):
    z, xh, y, core = (lax.axis_index(name) for name in ("z", "xh", "y", "core"))
    place = jnp.stack([y, 1 - 2 * core, lax.axis_index("xl"), xh, core]).astype(jnp.int32)
    right = lax.all_gather(vectors_right, "z", axis=0)
    t_own_split = split_amplitudes(amplitudes)
    same, other = send(vectors_left, SAME_XL), send(vectors_left, OTHER_XL)
    own = jnp.stack([after(same, t_own_split), other])
    x1 = send(own, RING_X)
    t_oth = send(amplitudes, SWAP_XH)
    y1 = send(own, RING_Y)
    own_swapped = send(own, SWAP_CORE)
    x2 = send(x1, RING_X)
    y2 = send(after(y1, x1), RING_Y)
    x1_swapped = send(after(x1, own_swapped), SWAP_CORE)
    x3 = send(after(x2, y1), RING_X)
    y3 = send(after(y2, x2), RING_Y)
    x4 = send(after(x3, y2), RING_X)
    t_split = (t_own_split, split_amplitudes(after(t_oth, x4)))
    left_own = [own, x1, x2, x3, x4, y3, y2, y1]
    x2_swapped = send(after(x2, x3, t_oth), SWAP_CORE)
    left_oth = [own_swapped, x1_swapped, x2_swapped] + [send(piece, SWAP_CORE) for piece in left_own[3:]]
    partial = contract(place, right, left_own, left_oth, t_split)
    near = lax.all_to_all(partial.reshape(64, 2, 128), ("xh", "xl", "y", "core"), 0, 0, tiled=True)
    near = jnp.broadcast_to(jnp.sum(near, axis=0), (8, 2, 128))
    far = jnp.sum(lax.all_to_all(near, "z", 0, 0, tiled=True), axis=0)
    return lax.dynamic_slice(far.reshape(4, 8, 8), (0, z, 0), (4, 1, 8)).reshape(4, 8, 1)


def solution(mesh):
    fine = Mesh(mesh.devices.reshape(SIZES), AXES)
    c_axes, d_axes = ("z", "xh"), ("xl", "y", "core")
    return jax.shard_map(
        shards,
        mesh=fine,
        in_specs=(P(None, c_axes, d_axes), P(None, d_axes, c_axes), P(c_axes, d_axes, None)),
        out_specs=P(d_axes, None, c_axes),
        check_vma=False,
    )
```

```python
import jax
import jax.numpy as jnp
from jax import lax
from jax.experimental import pallas as pl
from jax.experimental.pallas import tpu as pltpu
from jax.sharding import Mesh, PartitionSpec as P

AXES = ("z", "xh", "xl", "y", "core")
SIZES = (8, 2, 2, 8, 2)


def linear(z, xh, xl, y, core):
    return (((z % 8) * 2 + xh) * 2 + xl) * 16 + (y % 8) * 2 + core


def table(target):
    pairs = []
    for z in range(8):
        for xh in range(2):
            for xl in range(2):
                for y in range(8):
                    for core in range(2):
                        pairs.append((linear(z, xh, xl, y, core), linear(*target(z, xh, xl, y, core))))
    return pairs


SAME_XL = table(lambda z, xh, xl, y, core: (z, y % 2, xl, y // 2 * 2 + xh, core))
OTHER_XL = table(lambda z, xh, xl, y, core: (z, y % 2, 1 - xl, y // 2 * 2 + xh, core))
RING_X = table(lambda z, xh, xl, y, core: (z, xh, xl, y + 1 - 2 * core, core))
RING_Y = table(lambda z, xh, xl, y, core: (z, xh, xl, y - 1 + 2 * core, core))
SWAP_CORE = table(lambda z, xh, xl, y, core: (z, xh, xl, y, 1 - core))
SWAP_XH = table(lambda z, xh, xl, y, core: (z, 1 - xh, xl, y, core))
PAIRS = (0, 1, 3, 2)
GROUPS = ((0,), (1,), (7,), (2, 6), (3, 5), (4,))
NEEDED = ((0, 1, 7), (2, 6, 3, 5), (4,), ())


def send(array, pairs):
    return lax.ppermute(array, AXES, pairs)


def after(array, *earlier):
    return lax.optimization_barrier((array, *earlier))[0]


def split(value):
    high = value.astype(jnp.bfloat16)
    low = (value - high.astype(jnp.float32)).astype(jnp.bfloat16)
    return high, low


def dot_nt(a, b):
    return lax.dot_general(a, b, (((1,), (1,)), ((), ())), preferred_element_type=jnp.float32)


def dot_nn(a, b):
    return lax.dot_general(a, b, (((1,), (0,)), ((), ())), preferred_element_type=jnp.float32)


def amplitudes_kernel(block, out, raw, parts, sems):
    copy = pltpu.make_async_copy(block, raw, sems.at[0])
    copy.start()
    copy.wait()
    for d in range(32):
        high, low = split(raw[pl.ds(d, 64, 32), :])
        parts[0, d] = high
        parts[1, d] = low
    copy = pltpu.make_async_copy(parts, out, sems.at[1])
    copy.start()
    copy.wait()


def split_amplitudes(block, flops=1 << 20):
    return pl.pallas_call(
        amplitudes_kernel,
        out_shape=pltpu.HBM((2, 32, 64, 128), jnp.bfloat16),
        in_specs=[pl.BlockSpec(memory_space=pl.ANY)],
        out_specs=pl.BlockSpec(memory_space=pltpu.HBM),
        scratch_shapes=[
            pltpu.VMEM((2048, 128), jnp.float32),
            pltpu.VMEM((2, 32, 64, 128), jnp.bfloat16),
            pltpu.SemaphoreType.DMA((2,)),
        ],
        compiler_params=pltpu.CompilerParams(vmem_limit_bytes=8 * 1024 * 1024),
        cost_estimate=pl.CostEstimate(flops=flops, bytes_accessed=2 << 20, transcendentals=0),
        name="split_amplitudes",
    )(pltpu.with_memory_space_constraint(block.reshape(2048, 128), pltpu.HBM))


def ladder_kernel(place, right, *refs):
    own, oth, (t_own, t_oth, out) = refs[:8], refs[8:14], refs[14:17]
    swapped = {slot: ref.at[i] for group, ref in zip(GROUPS, oth) for i, slot in enumerate(group)}
    r_buf, raw, parts, t_buf, acc, y_high, y_low, flip, rows, r_sem, l_sem, t_sem = refs[17:]
    y, sign, xl_here, xh, core = (place[i] for i in range(5))

    def pair(k):
        return lax.rem(y // 2 + PAIRS[k], 4)

    def right_copy(k, order):
        where = lax.bitwise_xor(order, xl_here) * 4 + pair(k)
        return pltpu.make_async_copy(right.at[where], r_buf.at[k, order], r_sem.at[k, order])

    def left_copy(side, slot):
        return pltpu.make_async_copy(swapped[slot] if side else own[slot], raw.at[side, slot], l_sem.at[side, slot])

    def left(k, q_half, half, order):
        at = 2 * pair(k) + lax.bitwise_xor(half, xh)
        steps = (y - at) * sign
        side = lax.bitwise_xor(core, q_half)
        slot = lax.bitwise_and(8 + steps - 2 * side * steps, 7)
        return parts[side, slot, order]

    t_copies = [
        pltpu.make_async_copy(ref, t_buf.at[:, :, half], t_sem.at[half]) for half, ref in enumerate((t_own, t_oth))
    ]
    for k in range(4):
        for slot in NEEDED[k]:
            for side in range(2):
                left_copy(side, slot).start()
        for order in range(2):
            right_copy(k, order).start()
    for copy in t_copies:
        copy.start()
    for k in range(4):
        for slot in NEEDED[k]:
            for side in range(2):
                left_copy(side, slot).wait()
                high, low = split(raw[side, slot])
                parts[side, slot, :, :, :, :128] = high
                parts[side, slot, :, :, :, 128:] = low
        for order in range(2):
            right_copy(k, order).wait()
        r_high, r_low, l_high, l_low = [], [], [], []
        for order in range(2):
            high, low = split(r_buf[k, order].reshape(512, 256))
            r_high.append(high)
            r_low.append(low)
            for q_half in range(2):
                both = jnp.concatenate([left(k, q_half, half, order) for half in range(2)], axis=1).reshape(1024, 256)
                l_high.append(both[:, :128])
                l_low.append(both[:, 128:])
        product = dot_nt(
            jnp.concatenate(r_high + r_low + r_high, axis=1),
            jnp.concatenate(l_high + l_high + l_low, axis=1),
        )
        for a in range(8):
            piece = product[:, a * 128 : a * 128 + 128]
            if k == 0:
                acc[a] = piece
            else:
                acc[a] += piece
    for copy in t_copies:
        copy.wait()
    for d in range(32):
        for a in range(8):
            high, low = split(acc[a, pl.ds(d, 16, 32), :])
            y_high[a * 16 : a * 16 + 16, d * 128 : d * 128 + 128] = high
            y_low[a * 16 : a * 16 + 16, d * 128 : d * 128 + 128] = low
    t_high, t_low = (t_buf[i].reshape(4096, 128) for i in range(2))
    total = dot_nn(y_high[...], t_high) + dot_nn(y_high[...], t_low) + dot_nn(y_low[...], t_high)
    rows[...] = total
    for a in range(8):
        for xh_to in range(2):
            flip[pl.ds(xh_to * 64 + a, 8, 8), :] = rows[pl.ds(a * 16 + xh_to, 8, 2), :]
    rows[...] = flip[...].T
    even, odd = rows[pl.ds(0, 64, 2), :], rows[pl.ds(1, 64, 2), :]
    left_half = lax.broadcasted_iota(jnp.int32, (64, 128), 1) < 64
    out[0] = jnp.where(left_half, even, pltpu.roll(odd, 64, 1))
    out[1] = jnp.where(left_half, pltpu.roll(even, 64, 1), odd)


def contract(place, right, own, oth, t_split):
    return pl.pallas_call(
        ladder_kernel,
        out_shape=jax.ShapeDtypeStruct((2, 64, 128), jnp.float32),
        in_specs=[pl.BlockSpec(memory_space=pltpu.SMEM)] + [pl.BlockSpec(memory_space=pl.ANY)] * 17,
        out_specs=pl.BlockSpec(memory_space=pltpu.VMEM),
        scratch_shapes=[
            pltpu.VMEM((4, 2, 16, 32, 256), jnp.float32),
            pltpu.VMEM((2, 8, 2, 8, 64, 128), jnp.float32),
            pltpu.VMEM((2, 8, 2, 8, 64, 256), jnp.bfloat16),
            pltpu.VMEM((2, 32, 2, 64, 128), jnp.bfloat16),
            pltpu.VMEM((8, 512, 128), jnp.float32),
            pltpu.VMEM((128, 4096), jnp.bfloat16),
            pltpu.VMEM((128, 4096), jnp.bfloat16),
            pltpu.VMEM((128, 128), jnp.float32),
            pltpu.VMEM((128, 128), jnp.float32),
            pltpu.SemaphoreType.DMA((4, 2)),
            pltpu.SemaphoreType.DMA((2, 8)),
            pltpu.SemaphoreType.DMA((2,)),
        ],
        compiler_params=pltpu.CompilerParams(vmem_limit_bytes=60 * 1024 * 1024),
        cost_estimate=pl.CostEstimate(flops=6 << 30, bytes_accessed=16 << 20, transcendentals=0),
        name="ladder",
    )(place, right, *own, *oth, *t_split)


def shards(vectors_left, vectors_right, amplitudes):
    z, xh, y, core = (lax.axis_index(name) for name in ("z", "xh", "y", "core"))
    place = jnp.stack([y, 1 - 2 * core, lax.axis_index("xl"), xh, core]).astype(jnp.int32)
    right = lax.all_gather(vectors_right, "z", axis=0)
    t_own_split = split_amplitudes(amplitudes)
    same, other = send(vectors_left, SAME_XL), send(vectors_left, OTHER_XL)
    own = jnp.stack([after(same, t_own_split, place), other])
    x1 = send(own, RING_X)
    t_oth = send(amplitudes, SWAP_XH)
    y1 = send(own, RING_Y)
    own_swapped = send(own, SWAP_CORE)
    x2 = send(x1, RING_X)
    y2 = send(after(y1, x1), RING_Y)
    x1_swapped = send(after(x1, own_swapped), SWAP_CORE)
    x3 = send(after(x2, y1), RING_X)
    y3 = send(after(y2, x2), RING_Y)
    x4 = send(after(x3, y2), RING_X)
    t_split = (t_own_split, split_amplitudes(after(t_oth, x4), 30 << 30))
    left_own = [own, x1, x2, x3, x4, y3, y2, y1]
    left_oth = [
        own_swapped[None],
        x1_swapped[None],
        send(y1, SWAP_CORE)[None],
        send(after(jnp.stack([x2, y2]), x3, t_oth), SWAP_CORE),
        send(jnp.stack([x3, y3]), SWAP_CORE),
        send(x4, SWAP_CORE)[None],
    ]
    partial = contract(place, right, left_own, left_oth, t_split)
    near = lax.all_to_all(partial.reshape(64, 2, 128), ("xh", "xl", "y", "core"), 0, 0, tiled=True)
    near = jnp.broadcast_to(jnp.sum(near, axis=0), (8, 2, 128))
    far = jnp.sum(lax.all_to_all(near, "z", 0, 0, tiled=True), axis=0)
    return lax.dynamic_slice(far.reshape(4, 8, 8), (0, z, 0), (4, 1, 8)).reshape(4, 8, 1)


def solution(mesh):
    fine = Mesh(mesh.devices.reshape(SIZES), AXES)
    c_axes, d_axes = ("z", "xh"), ("xl", "y", "core")
    return jax.shard_map(
        shards,
        mesh=fine,
        in_specs=(P(None, c_axes, d_axes), P(None, d_axes, c_axes), P(c_axes, d_axes, None)),
        out_specs=P(d_axes, None, c_axes),
        check_vma=False,
    )
```

```python
import jax
import jax.numpy as jnp
from jax import lax
from jax.experimental import pallas as pl
from jax.experimental.pallas import tpu as pltpu
from jax.sharding import Mesh, PartitionSpec as P

AXES = ("z", "xh", "xl", "y", "core")
SIZES = (8, 2, 2, 8, 2)


def linear(z, xh, xl, y, core):
    return (((z % 8) * 2 + xh) * 2 + xl) * 16 + (y % 8) * 2 + core


def table(target):
    pairs = []
    for z in range(8):
        for xh in range(2):
            for xl in range(2):
                for y in range(8):
                    for core in range(2):
                        pairs.append((linear(z, xh, xl, y, core), linear(*target(z, xh, xl, y, core))))
    return pairs


SAME_XL = table(lambda z, xh, xl, y, core: (z, y % 2, xl, y // 2 * 2 + xh, core))
OTHER_XL = table(lambda z, xh, xl, y, core: (z, y % 2, 1 - xl, y // 2 * 2 + xh, core))
RING_X = table(lambda z, xh, xl, y, core: (z, xh, xl, y + 1 - 2 * core, core))
RING_Y = table(lambda z, xh, xl, y, core: (z, xh, xl, y - 1 + 2 * core, core))
SWAP_CORE = table(lambda z, xh, xl, y, core: (z, xh, xl, y, 1 - core))
SWAP_XH = table(lambda z, xh, xl, y, core: (z, 1 - xh, xl, y, core))
PAIRS = (0, 1, 3, 2)
NEEDED = ((0, 1, 7), (2, 6, 3, 5), (4,), ())


def send(array, pairs):
    return lax.ppermute(array, AXES, pairs)


def after(array, *earlier):
    return lax.optimization_barrier((array, *earlier))[0]


def split(value):
    high = value.astype(jnp.bfloat16)
    low = (value - high.astype(jnp.float32)).astype(jnp.bfloat16)
    return high, low


def dot_nt(a, b):
    return lax.dot_general(a, b, (((1,), (1,)), ((), ())), preferred_element_type=jnp.float32)


def dot_nn(a, b):
    return lax.dot_general(a, b, (((1,), (0,)), ((), ())), preferred_element_type=jnp.float32)


def amplitudes_kernel(block, out, raw, parts, sems):
    copy = pltpu.make_async_copy(block, raw, sems.at[0])
    copy.start()
    copy.wait()
    for d in range(32):
        high, low = split(raw[pl.ds(d, 64, 32), :])
        parts[0, d] = high
        parts[1, d] = low
    copy = pltpu.make_async_copy(parts, out, sems.at[1])
    copy.start()
    copy.wait()


def split_amplitudes(block):
    return pl.pallas_call(
        amplitudes_kernel,
        out_shape=pltpu.HBM((2, 32, 64, 128), jnp.bfloat16),
        in_specs=[pl.BlockSpec(memory_space=pl.ANY)],
        out_specs=pl.BlockSpec(memory_space=pltpu.HBM),
        scratch_shapes=[
            pltpu.VMEM((2048, 128), jnp.float32),
            pltpu.VMEM((2, 32, 64, 128), jnp.bfloat16),
            pltpu.SemaphoreType.DMA((2,)),
        ],
        compiler_params=pltpu.CompilerParams(vmem_limit_bytes=8 * 1024 * 1024),
        cost_estimate=pl.CostEstimate(flops=1 << 20, bytes_accessed=2 << 20, transcendentals=0),
        name="split_amplitudes",
    )(pltpu.with_memory_space_constraint(block.reshape(2048, 128), pltpu.HBM))


def ladder_kernel(place, right, *refs):
    pieces, (t_own, t_oth, out) = (refs[:8], refs[8:16]), refs[16:19]
    r_buf, raw, parts, t_buf, acc, y_high, y_low, flip, rows, r_sem, l_sem, t_sem = refs[19:]
    y, sign, xl_here, xh, core = (place[i] for i in range(5))

    def pair(k):
        return lax.rem(y // 2 + PAIRS[k], 4)

    def right_copy(k, order):
        where = lax.bitwise_xor(order, xl_here) * 4 + pair(k)
        return pltpu.make_async_copy(right.at[where], r_buf.at[k, order], r_sem.at[k, order])

    def left_copy(side, slot):
        return pltpu.make_async_copy(pieces[side][slot], raw.at[side, slot], l_sem.at[side, slot])

    def left(k, q_half, half, order):
        at = 2 * pair(k) + lax.bitwise_xor(half, xh)
        steps = (y - at) * sign
        side = lax.bitwise_xor(core, q_half)
        slot = lax.bitwise_and(8 + steps - 2 * side * steps, 7)
        return parts[side, slot, order]

    t_copies = [
        pltpu.make_async_copy(ref, t_buf.at[:, :, half], t_sem.at[half]) for half, ref in enumerate((t_own, t_oth))
    ]
    for k in range(4):
        for slot in NEEDED[k]:
            for side in range(2):
                left_copy(side, slot).start()
        for order in range(2):
            right_copy(k, order).start()
    for copy in t_copies:
        copy.start()
    for k in range(4):
        for slot in NEEDED[k]:
            for side in range(2):
                left_copy(side, slot).wait()
                high, low = split(raw[side, slot])
                parts[side, slot, :, :, :, :128] = high
                parts[side, slot, :, :, :, 128:] = low
        for order in range(2):
            right_copy(k, order).wait()
        r_high, r_low, l_high, l_low = [], [], [], []
        for order in range(2):
            high, low = split(r_buf[k, order].reshape(512, 256))
            r_high.append(high)
            r_low.append(low)
            for q_half in range(2):
                both = jnp.concatenate([left(k, q_half, half, order) for half in range(2)], axis=1).reshape(1024, 256)
                l_high.append(both[:, :128])
                l_low.append(both[:, 128:])
        product = dot_nt(
            jnp.concatenate(r_high + r_low + r_high, axis=1),
            jnp.concatenate(l_high + l_high + l_low, axis=1),
        )
        for a in range(8):
            piece = product[:, a * 128 : a * 128 + 128]
            if k == 0:
                acc[a] = piece
            else:
                acc[a] += piece
    for copy in t_copies:
        copy.wait()
    for d in range(32):
        for a in range(8):
            high, low = split(acc[a, pl.ds(d, 16, 32), :])
            y_high[a * 16 : a * 16 + 16, d * 128 : d * 128 + 128] = high
            y_low[a * 16 : a * 16 + 16, d * 128 : d * 128 + 128] = low
    t_high, t_low = (t_buf[i].reshape(4096, 128) for i in range(2))
    total = dot_nn(y_high[...], t_high) + dot_nn(y_high[...], t_low) + dot_nn(y_low[...], t_high)
    rows[...] = total
    for a in range(8):
        for xh_to in range(2):
            flip[pl.ds(xh_to * 64 + a, 8, 8), :] = rows[pl.ds(a * 16 + xh_to, 8, 2), :]
    rows[...] = flip[...].T
    even, odd = rows[pl.ds(0, 64, 2), :], rows[pl.ds(1, 64, 2), :]
    left_half = lax.broadcasted_iota(jnp.int32, (64, 128), 1) < 64
    out[0] = jnp.where(left_half, even, pltpu.roll(odd, 64, 1))
    out[1] = jnp.where(left_half, pltpu.roll(even, 64, 1), odd)


def contract(place, right, own, oth, t_split):
    return pl.pallas_call(
        ladder_kernel,
        out_shape=jax.ShapeDtypeStruct((2, 64, 128), jnp.float32),
        in_specs=[pl.BlockSpec(memory_space=pltpu.SMEM)] + [pl.BlockSpec(memory_space=pl.ANY)] * 19,
        out_specs=pl.BlockSpec(memory_space=pltpu.VMEM),
        scratch_shapes=[
            pltpu.VMEM((4, 2, 16, 32, 256), jnp.float32),
            pltpu.VMEM((2, 8, 2, 8, 64, 128), jnp.float32),
            pltpu.VMEM((2, 8, 2, 8, 64, 256), jnp.bfloat16),
            pltpu.VMEM((2, 32, 2, 64, 128), jnp.bfloat16),
            pltpu.VMEM((8, 512, 128), jnp.float32),
            pltpu.VMEM((128, 4096), jnp.bfloat16),
            pltpu.VMEM((128, 4096), jnp.bfloat16),
            pltpu.VMEM((128, 128), jnp.float32),
            pltpu.VMEM((128, 128), jnp.float32),
            pltpu.SemaphoreType.DMA((4, 2)),
            pltpu.SemaphoreType.DMA((2, 8)),
            pltpu.SemaphoreType.DMA((2,)),
        ],
        compiler_params=pltpu.CompilerParams(vmem_limit_bytes=60 * 1024 * 1024),
        cost_estimate=pl.CostEstimate(flops=6 << 30, bytes_accessed=16 << 20, transcendentals=0),
        name="ladder",
    )(place, right, *own, *oth, *t_split)


def shards(vectors_left, vectors_right, amplitudes):
    z, xh, y, core = (lax.axis_index(name) for name in ("z", "xh", "y", "core"))
    place = jnp.stack([y, 1 - 2 * core, lax.axis_index("xl"), xh, core]).astype(jnp.int32)
    right = lax.all_gather(vectors_right, "z", axis=0)
    t_own_split = split_amplitudes(amplitudes)
    same, other = send(vectors_left, SAME_XL), send(vectors_left, OTHER_XL)
    own = jnp.stack([after(same, t_own_split, place), other])
    x1 = send(own, RING_X)
    t_oth = send(amplitudes, SWAP_XH)
    y1 = send(own, RING_Y)
    own_swapped = send(own, SWAP_CORE)
    x2 = send(x1, RING_X)
    y2 = send(after(y1, x1), RING_Y)
    x1_swapped = send(after(x1, own_swapped), SWAP_CORE)
    x3 = send(after(x2, y1), RING_X)
    y3 = send(after(y2, x2), RING_Y)
    x4 = send(after(x3, y2), RING_X)
    t_split = (t_own_split, split_amplitudes(after(t_oth, x4)))
    left_own = [own, x1, x2, x3, x4, y3, y2, y1]
    x2_swapped = send(after(x2, x3, t_oth), SWAP_CORE)
    left_oth = [own_swapped, x1_swapped, x2_swapped] + [send(piece, SWAP_CORE) for piece in left_own[3:]]
    partial = contract(place, right, left_own, left_oth, t_split)
    near = lax.all_to_all(partial.reshape(64, 2, 128), ("xh", "xl", "y", "core"), 0, 0, tiled=True)
    near = jnp.broadcast_to(jnp.sum(near, axis=0), (8, 2, 128))
    far = jnp.sum(lax.all_to_all(near, "z", 0, 0, tiled=True), axis=0)
    return lax.dynamic_slice(far.reshape(4, 8, 8), (0, z, 0), (4, 1, 8)).reshape(4, 8, 1)


def solution(mesh):
    fine = Mesh(mesh.devices.reshape(SIZES), AXES)
    c_axes, d_axes = ("z", "xh"), ("xl", "y", "core")
    return jax.shard_map(
        shards,
        mesh=fine,
        in_specs=(P(None, c_axes, d_axes), P(None, d_axes, c_axes), P(c_axes, d_axes, None)),
        out_specs=P(d_axes, None, c_axes),
        check_vma=False,
    )
```
